512 devices in a mesh: group: 32 (over z_hi, x, core), loop: 16 (over y, z_lo).
Axes of the slice: x: 4, y: 8, z: 8 (z_hi: 4, z_lo: 2; z = z_hi * 2 + z_lo), core: 2. Of those that a mesh axis runs over, the one named last changes fastest.
Arguments:
- image_embed: bfloat16 [12288, 1152], P(('group', 'loop')), may hold values from -6 to 6
- text_embed: bfloat16 [12288, 1152], P(('group', 'loop')), may hold values from -6 to 6
- logit_scale: float32 [1], replicated, may hold values from 0.02 to 0.05
- logit_bias: float32 [1], replicated, may hold values from -4 to -1
Outputs:
- image_grad: float32 [12288, 1152], P(('group', 'loop'))
- text_grad: float32 [12288, 1152], P(('group', 'loop'))
The draws below stay inside these ranges and needn't reach their ends.
All inputs are finite; a program needn't handle non-finite values.
Results may differ from the reference program's by a relative error of at most 0.0013.
Values may be sent and summed in bfloat16 or wider, within the bound.
No kernel may reach another device: no remote copies, remote signals or barrier semaphores. Data moves between devices by JAX's collectives and lax.ppermute only.
A program may use at most 64 MiB of HBM per device.

```python
import jax
import jax.numpy as jnp
from jax import lax

D = 1152
ROWS = 24
PAIRS = 12288
N_GROUP = 32
N_LOOP = 16


def block_levels(key, extent, shards, least, high):
    def one(axis_at, shards_of):
        steps = jax.random.uniform(jax.random.fold_in(jax.random.fold_in(key, 6), axis_at), (shards_of,), jnp.float32, least / len(shards), high / len(shards))
        return jnp.repeat(jnp.exp(steps), extent[axis_at] // shards_of).reshape((-1,) + (1,) * (len(extent) - axis_at - 1))

    loudness = one(*shards[0])
    for cut in shards[1:]:
        loudness = loudness * one(*cut)
    return loudness


def gaussian(own_key, extent, scale, most, shards=(), kind=jnp.bfloat16):
    values = scale * jax.random.normal(own_key, extent, jnp.float32)
    if shards:
        values = values * block_levels(own_key, extent, shards, -0.22, 0.18)
    return jnp.clip(values, -most, most).astype(kind)


def setup_inputs(seed: int = 0) -> dict:
    keys = jax.random.split(jax.random.key(seed), 5)
    return {
        "image_embed": gaussian(keys[0], (PAIRS, D), 1.0, 6.0, ((0, 512),)),
        "text_embed": gaussian(keys[1], (PAIRS, D), 1.0, 6.0, ((0, 512),)),
        "logit_scale": jnp.clip(jax.random.uniform(keys[2], (1,), jnp.float32, 0.02, 0.05), 0.02, 0.05),
        "logit_bias": jnp.clip(jax.random.uniform(keys[3], (1,), jnp.float32, -4.0, -1.0), -4.0, -1.0),
    }


def reference(image_embed, text_embed, logit_scale, logit_bias):
    scale_value = logit_scale[0]
    bias_value = logit_bias[0]
    total_rows = image_embed.shape[0]
    block_rows = N_LOOP * ROWS
    text_blocks = text_embed.reshape(N_GROUP, block_rows, D)
    image_index = jnp.arange(total_rows, dtype=jnp.int32)

    def per_group(running, inputs):
        group_index, text_block = inputs
        products = lax.dot_general(text_block, image_embed, (((1,), (1,)), ((), ())), preferred_element_type=jnp.float32)
        logits = scale_value * products + bias_value
        text_index = group_index * block_rows + jnp.arange(block_rows, dtype=jnp.int32)
        labels = jnp.where(text_index[:, None] == image_index[None, :], jnp.float32(1.0), jnp.float32(-1.0))
        weight = (-labels * scale_value * jax.nn.sigmoid(-labels * logits)).astype(jnp.bfloat16)
        text_grad = jnp.dot(weight, image_embed, preferred_element_type=jnp.float32)
        partial_value = lax.dot_general(weight, text_block, (((0,), (0,)), ((), ())), preferred_element_type=jnp.float32)
        return running + partial_value, text_grad

    initial = jnp.zeros((total_rows, D), jnp.float32)
    image_grad, text_grads = lax.scan(per_group, initial, (jnp.arange(N_GROUP, dtype=jnp.int32), text_blocks))
    return image_grad, text_grads.reshape(total_rows, D)
```

```python
import jax
import jax.numpy as jnp
from jax import lax
from jax.experimental import pallas as pl
from jax.experimental.pallas import tpu as pltpu
from jax.sharding import Mesh, PartitionSpec as P

ROW_AXES = ("z_hi", "x")
LOOP_AXES = ("y", "z_lo")
LANES = 128


def finer_mesh(mesh):
    devices = mesh.devices.reshape(4, 4, 2, 8, 2)
    return Mesh(devices, ("z_hi", "x", "core", "y", "z_lo"))


def weights_of(text, image, scale_value, bias_value, same):
    products = lax.dot_general(
        text, image, (((1,), (1,)), ((), ())), preferred_element_type=jnp.float32
    )
    logits = scale_value * products + bias_value
    if same is None:
        return (scale_value / (1.0 + jnp.exp(-logits))).astype(jnp.bfloat16)
    magnitude = scale_value / (1.0 + jnp.exp(jnp.where(same, logits, -logits)))
    return jnp.where(same, -magnitude, magnitude).astype(jnp.bfloat16)


def pack_into(packed_ref, block, values):
    largest = jnp.max(jnp.abs(values), axis=-1, keepdims=True)
    power = jnp.floor(jnp.log2(jnp.maximum(largest, 2.0**-100)))
    width = values.shape[-1]
    packed_ref[block, :, :width] = values * jnp.exp2(13.0 - power)
    packed_ref[block, :, width:] = jnp.broadcast_to(power, (values.shape[0], LANES))


def own_kernel(place_ref, numbers_ref, text_ref, image_ref, text_part_ref, image_part_ref):
    rows = text_ref.shape[0]
    count = image_ref.shape[0]
    text_at = lax.broadcasted_iota(jnp.int32, (rows, count), 0) - place_ref[0]
    image_at = lax.broadcasted_iota(jnp.int32, (rows, count), 1) - place_ref[1]
    same = (text_at == image_at) & (text_at >= 0) & (text_at < place_ref[2])
    text = text_ref[...]
    image = image_ref[...]
    weight = weights_of(text, image, numbers_ref[0], numbers_ref[1], same)
    text_part_ref[...] = jnp.dot(weight, image, preferred_element_type=jnp.float32)
    image_part_ref[...] = lax.dot_general(
        weight, text, (((0,), (0,)), ((), ())), preferred_element_type=jnp.float32
    )


def other_kernel(
    numbers_ref, text_ref, image_ref, text_before_ref, packed_ref, image_part_ref, total_ref
):
    text = text_ref[...]
    image = image_ref[...]
    weight = weights_of(text, image, numbers_ref[0], numbers_ref[1], None)
    image_part_ref[...] = lax.dot_general(
        weight, text, (((0,), (0,)), ((), ())), preferred_element_type=jnp.float32
    )
    total_ref[...] = text_before_ref[...] + jnp.dot(
        weight, image, preferred_element_type=jnp.float32
    )
    blocks, rows, _ = packed_ref.shape
    for block in range(blocks):
        pack_into(packed_ref, block, total_ref[pl.ds(block * rows, rows), :])


def add_kernel(own_ref, arrived_ref, packed_ref):
    blocks, rows, _ = packed_ref.shape
    for block in range(blocks):
        part = pl.ds(block * rows, rows)
        pack_into(packed_ref, block, own_ref[part, :] + arrived_ref[part, :])


def sum_kernel(packed_ref, out_ref):
    width = out_ref.shape[-1]
    total = jnp.zeros(out_ref.shape, jnp.float32)
    for block in range(packed_ref.shape[0]):
        factor = jnp.exp2(packed_ref[block, :, width:] - 13.0)[:, :1]
        total = total + packed_ref[block, :, :width] * factor
    out_ref[...] = total


def spread(array, axes, count):
    return lax.all_to_all(
        jnp.broadcast_to(array[None], (count, *array.shape)), axes, 0, 0, tiled=True
    )


def exchange(packed, axes):
    arrived = lax.all_to_all(packed.astype(jnp.float16), axes, 0, 0, tiled=True)
    return arrived.astype(jnp.float32)


def local(image_embed, text_embed, logit_scale, logit_bias):
    row_count, feature_count = text_embed.shape
    row_places = lax.axis_size(ROW_AXES)
    loop_count = lax.axis_size(LOOP_AXES)
    row_place = lax.axis_index(ROW_AXES)
    loop_place = lax.axis_index(LOOP_AXES)
    swap = [(0, 1), (1, 0)]

    texts = spread(text_embed, LOOP_AXES, loop_count).reshape(-1, feature_count)
    images = spread(image_embed, ROW_AXES, row_places).reshape(-1, feature_count)
    other_images = lax.ppermute(images, "core", swap)
    numbers = jnp.concatenate([logit_scale, logit_bias])
    place = jnp.stack([loop_place * row_count, row_place * row_count, jnp.int32(row_count)])
    smem = pl.BlockSpec(memory_space=pltpu.SMEM)
    vmem = pl.BlockSpec(memory_space=pltpu.VMEM)
    text_rows, image_rows = texts.shape[0], images.shape[0]

    def call(kernel, name, in_specs, out_shape, *arguments, work=0, scratch=()):
        return pl.pallas_call(
            kernel,
            out_shape=out_shape,
            in_specs=in_specs,
            out_specs=jax.tree.map(lambda _: vmem, out_shape),
            scratch_shapes=scratch,
            compiler_params=pltpu.CompilerParams(vmem_limit_bytes=32 * 2**20),
            cost_estimate=pl.CostEstimate(
                flops=work * feature_count,
                bytes_accessed=4 * (text_rows + image_rows) * feature_count,
                transcendentals=work // 6,
            ),
            name=name,
        )(*arguments)

    def wide(*shape):
        return jax.ShapeDtypeStruct(shape, jnp.float32)

    text_shape = wide(text_rows, feature_count)
    image_shape = wide(image_rows, feature_count)
    result = wide(row_count, feature_count)
    work = 6 * text_rows * image_rows
    text_part, own_part = call(
        own_kernel, "own_block", [smem, smem, vmem, vmem], (text_shape, image_shape),
        place, numbers, texts, images, work=work,
    )
    text_packed, other_part = call(
        other_kernel, "other_block", [smem, vmem, vmem, vmem], (wide(loop_count, row_count, feature_count + LANES), image_shape),
        numbers, texts, other_images, text_part, work=work,
        scratch=[pltpu.VMEM(text_shape.shape, jnp.float32)],
    )
    arrived = lax.ppermute(other_part, "core", swap)
    text_arrived = exchange(text_packed, LOOP_AXES)
    text_out = call(sum_kernel, "text_sum", [vmem], result, text_arrived)
    image_packed = call(
        add_kernel, "image_pack", [vmem, vmem],
        wide(row_places, row_count, feature_count + LANES), own_part, arrived,
    )
    image_arrived = exchange(image_packed, ROW_AXES)
    image_out = call(sum_kernel, "image_sum", [vmem], result, image_arrived)
    return (image_out, text_out)


def solution(mesh):
    fine = finer_mesh(mesh)
    rows = P(("z_hi", "x", "core", "y", "z_lo"), None)
    return jax.shard_map(
        local, mesh=fine, in_specs=(rows, rows, P(), P()), out_specs=(rows, rows), check_vma=False
    )
```

```python
import functools

import jax
import jax.numpy as jnp
from jax import lax
from jax.experimental import pallas as pl
from jax.experimental.pallas import tpu as pltpu
from jax.sharding import Mesh, PartitionSpec as P

MESH_AXES = ("z_hi", "x", "core", "y", "z_lo")
TEXT_AXES = ("y", "z_lo")
LANES = 128
FOLD = 8


def finer_mesh(mesh):
    devices = mesh.devices.reshape(4, 4, 2, 8, 2)
    return Mesh(devices, MESH_AXES)


def weights_of(text, image, scale_value, bias_value, same):
    products = lax.dot_general(
        text, image, (((1,), (1,)), ((), ())), preferred_element_type=jnp.float32
    )
    logits = scale_value * products + bias_value
    if same is None:
        return (scale_value / (1.0 + jnp.exp(-logits))).astype(jnp.bfloat16)
    magnitude = scale_value / (1.0 + jnp.exp(jnp.where(same, logits, -logits)))
    return jnp.where(same, -magnitude, magnitude).astype(jnp.bfloat16)


def pack_into(packed_ref, block, values):
    rows, width = values.shape
    largest = jnp.max(jnp.abs(values), axis=-1, keepdims=True)
    power = jnp.floor(jnp.log2(jnp.maximum(largest, 2.0**-100)))
    scaled = values * jnp.exp2(13.0 - power)
    lane = lax.broadcasted_iota(jnp.int32, (FOLD, LANES), 1)
    tail = jnp.zeros((FOLD, LANES), jnp.float32)
    for k in range(rows // FOLD):
        part = slice(k * FOLD, (k + 1) * FOLD)
        packed_ref[block, :, k * width : (k + 1) * width] = scaled[part, :]
        tail = jnp.where(lane == k, power[part, :], tail)
    packed_ref[block, :, rows // FOLD * width :] = tail


def first_kernel(numbers_ref, text_ref, image_ref, text_part_ref, image_part_ref):
    text = text_ref[...]
    image = image_ref[...]
    weight = weights_of(text, image, numbers_ref[0], numbers_ref[1], None)
    image_part_ref[...] = lax.dot_general(
        weight, text, (((0,), (0,)), ((), ())), preferred_element_type=jnp.float32
    )
    text_part_ref[...] = jnp.dot(weight, image, preferred_element_type=jnp.float32)


def second_kernel(
    place_ref,
    numbers_ref,
    text_ref,
    image_ref,
    text_before_ref,
    packed_ref,
    image_part_ref,
    total_ref,
):
    rows = text_ref.shape[0]
    count = image_ref.shape[0]
    text_at = lax.broadcasted_iota(jnp.int32, (rows, count), 0) - place_ref[0]
    image_at = lax.broadcasted_iota(jnp.int32, (rows, count), 1)
    same = (text_at == image_at) & (text_at < place_ref[1])
    text = text_ref[...]
    image = image_ref[...]
    weight = weights_of(text, image, numbers_ref[0], numbers_ref[1], same)
    total_ref[...] = text_before_ref[...] + jnp.dot(
        weight, image, preferred_element_type=jnp.float32
    )
    blocks = packed_ref.shape[0]
    block_rows = rows // blocks
    for block in range(blocks):
        pack_into(packed_ref, block, total_ref[pl.ds(block * block_rows, block_rows), :])
    image_part_ref[...] = lax.dot_general(
        weight, text, (((0,), (0,)), ((), ())), preferred_element_type=jnp.float32
    )


def unpacked(packed_ref, block, width, k):
    folds = (packed_ref.shape[-1] - LANES) // width
    factor = jnp.exp2(packed_ref[block, :, folds * width :] - 13.0)[:, k : k + 1]
    return packed_ref[block, :, k * width : (k + 1) * width] * factor


def add_kernel(own_ref, arrived_ref, kept_ref, *packed_refs):
    kept_rows = kept_ref.shape[0]
    kept = pl.ds(0, kept_rows)
    kept_ref[...] = own_ref[kept, :] + arrived_ref[kept, :]
    blocks = packed_refs[0].shape[0]
    block_rows = kept_rows // blocks
    for place, packed_ref in enumerate(packed_refs):
        for block in range(blocks):
            part = pl.ds((place + 1) * kept_rows + block * block_rows, block_rows)
            pack_into(packed_ref, block, own_ref[part, :] + arrived_ref[part, :])


def middle_kernel(places, *refs):
    before_ref, arrived_refs = refs[0], refs[1:places]
    kept_ref, packed_refs = refs[places], refs[places + 1 :]
    width = before_ref.shape[-1]
    block_rows = kept_ref.shape[0]
    for block in range(len(packed_refs) + 1):
        stretches = []
        for k in range(block_rows // FOLD):
            total = before_ref[pl.ds(block * block_rows + k * FOLD, FOLD), :]
            for arrived_ref in arrived_refs:
                total = total + unpacked(arrived_ref, block, width, k)
            stretches.append(total)
        total = jnp.concatenate(stretches, axis=0)
        if block == 0:
            kept_ref[...] = total
        else:
            pack_into(packed_refs[block - 1], 0, total)


def last_kernel(*refs):
    before_ref, arrived_refs, out_ref = refs[0], refs[1:-1], refs[-1]
    rows, width = out_ref.shape
    for k in range(rows // FOLD):
        part = pl.ds(k * FOLD, FOLD)
        total = before_ref[part, :]
        for arrived_ref in arrived_refs:
            total = total + unpacked(arrived_ref, 0, width, k)
        out_ref[part, :] = total


def sum_kernel(packed_ref, out_ref):
    rows, width = out_ref.shape
    for k in range(rows // FOLD):
        total = unpacked(packed_ref, 0, width, k)
        for block in range(1, packed_ref.shape[0]):
            total = total + unpacked(packed_ref, block, width, k)
        out_ref[pl.ds(k * FOLD, FOLD), :] = total


def spread(array, axes, count):
    return lax.all_to_all(
        jnp.broadcast_to(array[None], (count, *array.shape)), axes, 0, 0, tiled=True
    )


def exchange(packed, axes):
    arrived = lax.all_to_all(packed.astype(jnp.float16), axes, 0, 0, tiled=True)
    return arrived.astype(jnp.float32)


def gather_ring(array, axis):
    size = lax.axis_size(axis)
    others = [
        lax.ppermute(array, axis, [((i + k) % size, i) for i in range(size)])
        for k in range(1, size)
    ]
    return jnp.concatenate([array, *others], axis=0)


def send_ring(packed, axis):
    size = lax.axis_size(axis)
    return [
        lax.ppermute(
            array.astype(jnp.float16), axis, [(i, (i + k) % size) for i in range(size)]
        ).astype(jnp.float32)
        for k, array in enumerate(packed, 1)
    ]


def local(image_embed, text_embed, logit_scale, logit_bias):
    row_count, feature_count = text_embed.shape
    text_places = lax.axis_size(TEXT_AXES)
    x_places, z_places = lax.axis_size("x"), lax.axis_size("z_hi")
    text_place = lax.axis_index(TEXT_AXES)
    swap = [(0, 1), (1, 0)]

    texts = spread(text_embed, TEXT_AXES, text_places).reshape(-1, feature_count)
    images = gather_ring(gather_ring(image_embed, "z_hi"), "x")
    other_images = lax.ppermute(images, "core", swap)
    numbers = jnp.concatenate([logit_scale, logit_bias])
    place = jnp.stack([text_place * row_count, jnp.int32(row_count)])
    smem = pl.BlockSpec(memory_space=pltpu.SMEM)
    vmem = pl.BlockSpec(memory_space=pltpu.VMEM)
    text_rows, image_rows = texts.shape[0], images.shape[0]

    def call(kernel, name, in_specs, out_shape, *arguments, work=0, scratch=()):
        return pl.pallas_call(
            kernel,
            out_shape=out_shape,
            in_specs=in_specs,
            out_specs=jax.tree.map(lambda _: vmem, out_shape),
            scratch_shapes=scratch,
            compiler_params=pltpu.CompilerParams(vmem_limit_bytes=32 * 2**20),
            cost_estimate=pl.CostEstimate(
                flops=work * feature_count,
                bytes_accessed=4 * (text_rows + image_rows) * feature_count,
                transcendentals=work // 6,
            ),
            name=name,
        )(*arguments)

    def wide(*shape):
        return jax.ShapeDtypeStruct(shape, jnp.float32)

    def packed(places):
        return wide(places, FOLD, row_count // FOLD * feature_count + LANES)

    text_shape = wide(text_rows, feature_count)
    image_shape = wide(image_rows, feature_count)
    result = wide(row_count, feature_count)
    work = 6 * text_rows * image_rows
    text_part, other_part = call(
        first_kernel, "other_block", [smem, vmem, vmem], (text_shape, image_shape),
        numbers, texts, other_images, work=work,
    )
    arrived = lax.ppermute(other_part, "core", swap)
    text_packed, own_part = call(
        second_kernel, "own_block", [smem, smem, vmem, vmem, vmem],
        (packed(text_places), image_shape), place, numbers, texts, images, text_part,
        work=work, scratch=[pltpu.VMEM(text_shape.shape, jnp.float32)],
    )
    text_arrived = exchange(text_packed, TEXT_AXES)
    text_out = call(sum_kernel, "text_sum", [vmem], result, text_arrived)
    kept, *packed_x = call(
        add_kernel, "image_x", [vmem, vmem],
        (wide(z_places * row_count, feature_count), *[packed(z_places)] * (x_places - 1)),
        own_part, arrived,
    )
    kept, *packed_z = call(
        functools.partial(middle_kernel, x_places), "image_z", [vmem] * x_places, (result, *[packed(1)] * (z_places - 1)),
        kept, *send_ring(packed_x, "x"),
    )
    image_out = call(
        last_kernel, "image_sum", [vmem] * z_places, result, kept, *send_ring(packed_z, "z_hi")
    )
    return (image_out, text_out)


def solution(mesh):
    fine = finer_mesh(mesh)
    rows = P(MESH_AXES, None)
    return jax.shard_map(
        local, mesh=fine, in_specs=(rows, rows, P(), P()), out_specs=(rows, rows), check_vma=False
    )
```

```python
import jax
import jax.numpy as jnp
from jax import lax
from jax.experimental import pallas as pl
from jax.experimental.pallas import tpu as pltpu
from jax.sharding import Mesh, PartitionSpec as P

MESH_AXES = ("z_hi", "x", "core", "y", "z_lo")
TEXT_AXES = ("y", "z_lo")
LANES = 128
FOLD = 8


def finer_mesh(mesh):
    devices = mesh.devices.reshape(4, 4, 2, 8, 2)
    return Mesh(devices, MESH_AXES)


def weights_of(text, image, scale_value, bias_value, same):
    products = lax.dot_general(
        text, image, (((1,), (1,)), ((), ())), preferred_element_type=jnp.float32
    )
    logits = scale_value * products + bias_value
    if same is None:
        return (scale_value / (1.0 + jnp.exp(-logits))).astype(jnp.bfloat16)
    count = same.shape[1]
    first = logits[:, :count]
    magnitude = scale_value / (1.0 + jnp.exp(jnp.where(same, first, -first)))
    weight = jnp.where(same, -magnitude, magnitude)
    if count < logits.shape[1]:
        rest = scale_value / (1.0 + jnp.exp(-logits[:, count:]))
        weight = jnp.concatenate([weight, rest], axis=1)
    return weight.astype(jnp.bfloat16)


def pack_into(packed_ref, block, values):
    rows, width = values.shape
    largest = jnp.max(jnp.abs(values), axis=-1, keepdims=True)
    power = jnp.floor(jnp.log2(jnp.maximum(largest, 2.0**-100)))
    scaled = values * jnp.exp2(13.0 - power)
    lane = lax.broadcasted_iota(jnp.int32, (FOLD, LANES), 1)
    tail = jnp.zeros((FOLD, LANES), jnp.float32)
    for k in range(rows // FOLD):
        part = slice(k * FOLD, (k + 1) * FOLD)
        packed_ref[block, :, k * width : (k + 1) * width] = scaled[part, :]
        tail = jnp.where(lane == k, power[part, :], tail)
    packed_ref[block, :, rows // FOLD * width :] = tail


def block_kernel(
    place_ref,
    numbers_ref,
    text_ref,
    own_ref,
    other_ref,
    packed_ref,
    own_part_ref,
    other_part_ref,
    total_ref,
):
    rows = text_ref.shape[0]
    scale_value, bias_value = numbers_ref[0], numbers_ref[1]
    text = text_ref[...]

    def back(weight):
        return lax.dot_general(
            weight, text, (((0,), (0,)), ((), ())), preferred_element_type=jnp.float32
        )

    other = other_ref[...]
    weight = weights_of(text, other, scale_value, bias_value, None)
    other_part_ref[...] = back(weight)
    total_ref[...] = jnp.dot(weight, other, preferred_element_type=jnp.float32)

    own = own_ref[...]
    count = min(LANES, own.shape[0])
    text_at = lax.broadcasted_iota(jnp.int32, (rows, count), 0) - place_ref[0]
    image_at = lax.broadcasted_iota(jnp.int32, (rows, count), 1) - place_ref[1]
    same = (text_at == image_at) & (text_at >= 0) & (text_at < place_ref[2])
    weight = weights_of(text, own, scale_value, bias_value, same)
    own_part_ref[...] = back(weight)
    total_ref[...] += jnp.dot(weight, own, preferred_element_type=jnp.float32)
    blocks = packed_ref.shape[0]
    block_rows = rows // blocks
    for block in range(blocks):
        pack_into(packed_ref, block, total_ref[pl.ds(block * block_rows, block_rows), :])


def unpacked(packed_ref, block, width, k):
    folds = (packed_ref.shape[-1] - LANES) // width
    factor = jnp.exp2(packed_ref[block, :, folds * width :] - 13.0)[:, k : k + 1]
    return packed_ref[block, :, k * width : (k + 1) * width] * factor


def add_kernel(own_ref, arrived_ref, kept_ref, *packed_refs):
    kept_rows = kept_ref.shape[0]
    kept = pl.ds(0, kept_rows)
    kept_ref[...] = own_ref[kept, :] + arrived_ref[kept, :]
    blocks = packed_refs[0].shape[0]
    block_rows = kept_rows // blocks
    for place, packed_ref in enumerate(packed_refs):
        for block in range(blocks):
            part = pl.ds((place + 1) * kept_rows + block * block_rows, block_rows)
            pack_into(packed_ref, block, own_ref[part, :] + arrived_ref[part, :])


def middle_kernel(*refs):
    before_ref, arrived_refs, packed_ref = refs[0], refs[1:-1], refs[-1]
    width = before_ref.shape[-1]
    blocks = packed_ref.shape[0]
    block_rows = before_ref.shape[0] // blocks
    for block in range(blocks):
        stretches = []
        for k in range(block_rows // FOLD):
            total = before_ref[pl.ds(block * block_rows + k * FOLD, FOLD), :]
            for arrived_ref in arrived_refs:
                total = total + unpacked(arrived_ref, block, width, k)
            stretches.append(total)
        pack_into(packed_ref, block, jnp.concatenate(stretches, axis=0))


def sum_kernel(packed_ref, out_ref):
    rows, width = out_ref.shape
    for k in range(rows // FOLD):
        total = unpacked(packed_ref, 0, width, k)
        for block in range(1, packed_ref.shape[0]):
            total = total + unpacked(packed_ref, block, width, k)
        out_ref[pl.ds(k * FOLD, FOLD), :] = total


def spread(array, axes, count):
    return lax.all_to_all(
        jnp.broadcast_to(array[None], (count, *array.shape)), axes, 0, 0, tiled=True
    )


def exchange(packed, axes):
    arrived = lax.all_to_all(packed.astype(jnp.float16), axes, 0, 0, tiled=True)
    return arrived.astype(jnp.float32)


def gather_ring(array, axis):
    size = lax.axis_size(axis)
    others = [
        lax.ppermute(array, axis, [((i + k) % size, i) for i in range(size)])
        for k in range(1, size)
    ]
    return jnp.concatenate([array, *others], axis=0)


def send_ring(packed, axis):
    size = lax.axis_size(axis)
    return [
        lax.ppermute(
            array.astype(jnp.float16), axis, [(i, (i + k) % size) for i in range(size)]
        ).astype(jnp.float32)
        for k, array in enumerate(packed, 1)
    ]


def local(image_embed, text_embed, logit_scale, logit_bias):
    row_count, feature_count = text_embed.shape
    text_places = lax.axis_size(TEXT_AXES)
    x_places, z_places = lax.axis_size("x"), lax.axis_size("z_hi")
    text_place, z_place = lax.axis_index(TEXT_AXES), lax.axis_index("z_hi")
    swap = [(0, 1), (1, 0)]

    texts = spread(text_embed, TEXT_AXES, text_places).reshape(-1, feature_count)
    column = spread(image_embed, "z_hi", z_places).reshape(-1, feature_count)
    images = gather_ring(column, "x")
    other_images = lax.ppermute(images, "core", swap)
    numbers = jnp.concatenate([logit_scale, logit_bias])
    place = jnp.stack([text_place * row_count, z_place * row_count, jnp.int32(row_count)])
    smem = pl.BlockSpec(memory_space=pltpu.SMEM)
    vmem = pl.BlockSpec(memory_space=pltpu.VMEM)
    text_rows, image_rows = texts.shape[0], images.shape[0]

    def call(kernel, name, in_specs, out_shape, *arguments, work=0, scratch=()):
        return pl.pallas_call(
            kernel,
            out_shape=out_shape,
            in_specs=in_specs,
            out_specs=jax.tree.map(lambda _: vmem, out_shape),
            scratch_shapes=scratch,
            compiler_params=pltpu.CompilerParams(vmem_limit_bytes=24 * 2**20),
            cost_estimate=pl.CostEstimate(
                flops=work * feature_count,
                bytes_accessed=4 * (text_rows + image_rows) * feature_count,
                transcendentals=work // 6,
            ),
            name=name,
        )(*arguments)

    def wide(*shape):
        return jax.ShapeDtypeStruct(shape, jnp.float32)

    def packed(places):
        return wide(places, FOLD, row_count // FOLD * feature_count + LANES)

    text_shape = wide(text_rows, feature_count)
    image_shape = wide(image_rows, feature_count)
    result = wide(row_count, feature_count)
    text_packed, own_part, other_part = call(
        block_kernel, "block", [smem, smem, vmem, vmem, vmem],
        (packed(text_places), image_shape, image_shape),
        place, numbers, texts, images, other_images,
        work=12 * text_rows * image_rows, scratch=[pltpu.VMEM(text_shape.shape, jnp.float32)],
    )
    arrived = lax.ppermute(other_part, "core", swap)
    text_arrived = exchange(text_packed, TEXT_AXES)
    text_out = call(sum_kernel, "text_sum", [vmem], result, text_arrived)
    kept, *packed_x = call(
        add_kernel, "image_x", [vmem, vmem],
        (wide(z_places * row_count, feature_count), *[packed(z_places)] * (x_places - 1)),
        own_part, arrived,
    )
    packed_z = call(
        middle_kernel, "image_z", [vmem] * x_places, packed(z_places),
        kept, *send_ring(packed_x, "x"),
    )
    image_out = call(sum_kernel, "image_sum", [vmem], result, exchange(packed_z, "z_hi"))
    return (image_out, text_out)


def solution(mesh):
    fine = finer_mesh(mesh)
    rows = P(MESH_AXES, None)
    return jax.shard_map(
        local, mesh=fine, in_specs=(rows, rows, P(), P()), out_specs=(rows, rows), check_vma=False
    )
```

```python
import jax
import jax.numpy as jnp
import numpy as np
from jax import lax
from jax.experimental import pallas as pl
from jax.experimental.pallas import tpu as pltpu
from jax.sharding import Mesh, PartitionSpec as P

MESH_AXES = ("z_hi", "x_hi", "x_lo", "core", "y", "z_lo")
IMAGE_AXES = ("x_lo", "z_hi", "z_lo")
TEXT_AXES = ("x_hi", "y")
LANES = 128
FOLD = 8


def finer_mesh(mesh):
    return Mesh(mesh.devices.reshape(4, 2, 2, 2, 8, 2), MESH_AXES)


def exchange_groups(sizes):
    places = np.arange(np.prod(sizes)).reshape(sizes)
    groups = []
    for core, axes in enumerate((IMAGE_AXES, TEXT_AXES)):
        part = np.take(places, core, axis=MESH_AXES.index("core"))
        names = [name for name in MESH_AXES if name != "core"]
        fixed = [name for name in names if name not in axes]
        order = [names.index(name) for name in (*fixed, *axes)]
        length = np.prod([sizes[MESH_AXES.index(name)] for name in axes])
        groups += part.transpose(order).reshape(-1, length).tolist()
    return groups


def weights_of(mine, other, scale_value, bias_value, same=None):
    products = lax.dot_general(
        mine, other, (((1,), (1,)), ((), ())), preferred_element_type=jnp.float32
    )
    logits = scale_value * products + bias_value
    if same is None:
        return (scale_value / (1.0 + jnp.exp(-logits))).astype(jnp.bfloat16)
    magnitude = scale_value / (1.0 + jnp.exp(jnp.where(same, logits, -logits)))
    return jnp.where(same, -magnitude, magnitude).astype(jnp.bfloat16)


def pack_into(packed_ref, block, values):
    rows, width = values.shape
    largest = jnp.max(jnp.abs(values), axis=-1, keepdims=True)
    power = jnp.floor(jnp.log2(jnp.maximum(largest, 2.0**-100)))
    scaled = values * jnp.exp2(13.0 - power)
    lane = lax.broadcasted_iota(jnp.int32, (FOLD, LANES), 1)
    tail = jnp.zeros((FOLD, LANES), jnp.float32)
    for k in range(rows // FOLD):
        part = slice(k * FOLD, (k + 1) * FOLD)
        packed_ref[block, :, k * width : (k + 1) * width] = scaled[part, :]
        tail = jnp.where(lane == k, power[part, :], tail)
    packed_ref[block, :, rows // FOLD * width :] = tail


def block_kernel(chip_rows, place_ref, numbers_ref, mine_ref, other_ref, packed_ref, total_ref):
    rows = mine_ref.shape[0]
    scale_value, bias_value = numbers_ref[0], numbers_ref[1]
    other = other_ref[...]
    step = rows // 3
    for start in range(0, rows, step):
        part = pl.ds(start, step)
        weight = weights_of(mine_ref[part, :], other, scale_value, bias_value)
        total_ref[part, :] = jnp.dot(weight, other, preferred_element_type=jnp.float32)

    shape = (chip_rows, other.shape[0])
    band = pl.ds(pl.multiple_of(place_ref[0] * chip_rows, 16), chip_rows)
    row = lax.broadcasted_iota(jnp.int32, shape, 0)
    column = lax.broadcasted_iota(jnp.int32, shape, 1) - place_ref[1] * chip_rows
    weight = weights_of(mine_ref[band, :], other, scale_value, bias_value, row == column)
    total_ref[band, :] = jnp.dot(weight, other, preferred_element_type=jnp.float32)

    blocks = packed_ref.shape[0]
    block_rows = rows // blocks
    for block in range(blocks):
        pack_into(packed_ref, block, total_ref[pl.ds(block * block_rows, block_rows), :])


def sum_kernel(core_ref, packed_ref, own_ref, sent_ref):
    rows, width = own_ref.shape
    folds = rows // FOLD
    for out_ref, core in ((own_ref, core_ref[0]), (sent_ref, 1 - core_ref[0])):
        for k in range(folds):
            total = jnp.zeros((FOLD, width), jnp.float32)
            for place in range(packed_ref.shape[0] // 2):
                block = 2 * place + core
                factor = jnp.exp2(packed_ref[block, :, folds * width :] - 13.0)[:, k : k + 1]
                total = total + packed_ref[block, :, k * width : (k + 1) * width] * factor
            out_ref[pl.ds(k * FOLD, FOLD), :] = total


def local(image_embed, text_embed, logit_scale, logit_bias):
    row_count, feature_count = text_embed.shape
    sizes = tuple(lax.axis_size(name) for name in MESH_AXES)
    groups = exchange_groups(sizes)
    places = len(groups[0])
    core = lax.axis_index("core")
    image_core = core == 0
    swap = [(0, 1), (1, 0)]

    def exchange(array):
        return lax.all_to_all(
            array, MESH_AXES, 0, 0, axis_index_groups=groups, tiled=True
        )

    kept = jnp.where(image_core, image_embed, text_embed)
    arrived = lax.ppermute(jnp.where(image_core, text_embed, image_embed), "core", swap)
    chip = jnp.concatenate(
        [jnp.where(image_core, kept, arrived), jnp.where(image_core, arrived, kept)], axis=0
    )
    mine = exchange(jnp.broadcast_to(chip[None], (places, *chip.shape)))
    mine = mine.reshape(-1, feature_count)
    other = lax.ppermute(mine, "core", swap)

    numbers = jnp.concatenate([logit_scale, logit_bias])
    image_place, text_place = lax.axis_index(IMAGE_AXES), lax.axis_index(TEXT_AXES)
    place = jnp.where(
        image_core, jnp.stack([image_place, text_place]), jnp.stack([text_place, image_place])
    )
    smem = pl.BlockSpec(memory_space=pltpu.SMEM)
    vmem = pl.BlockSpec(memory_space=pltpu.VMEM)
    params = pltpu.CompilerParams(vmem_limit_bytes=24 * 2**20)
    rows = mine.shape[0]
    width = row_count // FOLD * feature_count + LANES
    packed = pl.pallas_call(
        lambda *refs: block_kernel(2 * row_count, *refs),
        out_shape=jax.ShapeDtypeStruct((2 * places, FOLD, width), jnp.float32),
        in_specs=[smem, smem, vmem, vmem],
        out_specs=vmem,
        scratch_shapes=[pltpu.VMEM((rows, feature_count), jnp.float32)],
        compiler_params=params,
        cost_estimate=pl.CostEstimate(
            flops=4 * rows * rows * feature_count,
            bytes_accessed=8 * rows * feature_count,
            transcendentals=rows * rows,
        ),
        name="block",
    )(place, numbers, mine, other)
    sums = exchange(packed.astype(jnp.float16)).astype(jnp.float32)
    result = jax.ShapeDtypeStruct((row_count, feature_count), jnp.float32)
    own, sent = pl.pallas_call(
        sum_kernel,
        out_shape=(result, result),
        in_specs=[smem, vmem],
        out_specs=(vmem, vmem),
        compiler_params=params,
        cost_estimate=pl.CostEstimate(
            flops=4 * rows * feature_count,
            bytes_accessed=4 * rows * feature_count,
            transcendentals=0,
        ),
        name="sum_parts",
    )(core[None], sums)
    sibling = lax.ppermute(sent, "core", swap)
    return (jnp.where(image_core, own, sibling), jnp.where(image_core, sibling, own))


def solution(mesh):
    rows = P(MESH_AXES, None)
    return jax.shard_map(
        local,
        mesh=finer_mesh(mesh),
        in_specs=(rows, rows, P(), P()),
        out_specs=(rows, rows),
        check_vma=False,
    )
```

```python
import jax
import jax.numpy as jnp
import numpy as np
from jax import lax
from jax.experimental import pallas as pl
from jax.experimental.pallas import tpu as pltpu
from jax.sharding import Mesh, PartitionSpec as P

MESH_AXES = ("z_hi", "x", "core", "y", "z_lo")
IMAGE_AXES = ("z_hi", "z_lo")
TEXT_AXES = ("y",)
LANES = 128
FOLD = 8


def finer_mesh(mesh):
    return Mesh(mesh.devices.reshape(4, 4, 2, 8, 2), MESH_AXES)


def exchange_groups(sizes):
    places = np.arange(np.prod(sizes)).reshape(sizes)
    groups = []
    for core, axes in enumerate((IMAGE_AXES, TEXT_AXES)):
        part = np.take(places, core, axis=MESH_AXES.index("core"))
        names = [name for name in MESH_AXES if name != "core"]
        fixed = [name for name in names if name not in axes]
        order = [names.index(name) for name in (*fixed, *axes)]
        length = np.prod([sizes[MESH_AXES.index(name)] for name in axes])
        groups += part.transpose(order).reshape(-1, length).tolist()
    return groups


def x_pairs(count):
    pairs = []
    for x in range(count):
        for core in range(2):
            step = 1 if (x + core) % 2 == 0 else -1
            pairs.append((2 * x + core, 2 * ((x + step) % count) + core))
    return pairs


def weights_of(mine, other, scale_value, bias_value, same=None):
    products = lax.dot_general(
        mine, other, (((1,), (1,)), ((), ())), preferred_element_type=jnp.float32
    )
    logits = scale_value * products + bias_value
    if same is None:
        return (scale_value / (1.0 + jnp.exp(-logits))).astype(jnp.bfloat16)
    magnitude = scale_value / (1.0 + jnp.exp(jnp.where(same, logits, -logits)))
    return jnp.where(same, -magnitude, magnitude).astype(jnp.bfloat16)


def pack_into(packed_ref, block, values):
    rows, width = values.shape
    largest = jnp.max(jnp.abs(values), axis=-1, keepdims=True)
    power = jnp.floor(jnp.log2(jnp.maximum(largest, 2.0**-100)))
    scaled = values * jnp.exp2(13.0 - power)
    lane = lax.broadcasted_iota(jnp.int32, (FOLD, LANES), 1)
    tail = jnp.zeros((FOLD, LANES), jnp.float32)
    for k in range(rows // FOLD):
        part = slice(k * FOLD, (k + 1) * FOLD)
        packed_ref[block, :, k * width : (k + 1) * width] = scaled[part, :]
        tail = jnp.where(lane == k, power[part, :], tail)
    packed_ref[block, :, rows // FOLD * width :] = tail


def near_kernel(chip_rows, place_ref, numbers_ref, mine_ref, other_ref, out_ref):
    scale_value, bias_value = numbers_ref[0], numbers_ref[1]
    other = other_ref[...]
    weight = weights_of(mine_ref[...], other, scale_value, bias_value)
    out_ref[...] = jnp.dot(weight, other, preferred_element_type=jnp.float32)

    shape = (chip_rows, other.shape[0])
    band = pl.ds(pl.multiple_of(place_ref[0] * chip_rows, 16), chip_rows)
    row = lax.broadcasted_iota(jnp.int32, shape, 0)
    column = lax.broadcasted_iota(jnp.int32, shape, 1) - place_ref[1] * chip_rows
    weight = weights_of(mine_ref[band, :], other, scale_value, bias_value, row == column)
    out_ref[band, :] = jnp.dot(weight, other, preferred_element_type=jnp.float32)


def far_kernel(numbers_ref, mine_ref, near_ref, far_ref, packed_ref, total_ref):
    scale_value, bias_value = numbers_ref[0], numbers_ref[1]
    mine, near, far = mine_ref[...], near_ref[...], far_ref[...]
    weight = weights_of(mine, near, scale_value, bias_value)
    total_ref[...] = jnp.dot(weight, near, preferred_element_type=jnp.float32)
    weight = weights_of(mine, far, scale_value, bias_value)
    total_ref[...] += jnp.dot(weight, far, preferred_element_type=jnp.float32)
    blocks = packed_ref.shape[0]
    block_rows = mine.shape[0] // blocks
    for block in range(blocks):
        pack_into(packed_ref, block, total_ref[pl.ds(block * block_rows, block_rows), :])


def rest_kernel(numbers_ref, mine_ref, other_ref, before_ref, out_ref):
    other = other_ref[...]
    weight = weights_of(mine_ref[...], other, numbers_ref[0], numbers_ref[1])
    out_ref[...] = before_ref[...] + jnp.dot(weight, other, preferred_element_type=jnp.float32)


def unpacked(packed_ref, block, width, k):
    folds = (packed_ref.shape[-1] - LANES) // width
    factor = jnp.exp2(packed_ref[block, :, folds * width :] - 13.0)[:, k : k + 1]
    return packed_ref[block, :, k * width : (k + 1) * width] * factor


def add_kernel(before_ref, arrived_ref, packed_ref):
    rows, width = before_ref.shape
    blocks = packed_ref.shape[0]
    block_rows = rows // blocks
    for block in range(blocks):
        stretches = [
            before_ref[pl.ds(block * block_rows + k * FOLD, FOLD), :]
            + unpacked(arrived_ref, block, width, k)
            for k in range(block_rows // FOLD)
        ]
        pack_into(packed_ref, block, jnp.concatenate(stretches, axis=0))


def sum_kernel(core_ref, packed_ref, own_ref, sent_ref):
    rows, width = own_ref.shape
    for out_ref, core in ((own_ref, core_ref[0]), (sent_ref, 1 - core_ref[0])):
        for k in range(rows // FOLD):
            total = jnp.zeros((FOLD, width), jnp.float32)
            for place in range(packed_ref.shape[0] // 2):
                total = total + unpacked(packed_ref, 2 * place + core, width, k)
            out_ref[pl.ds(k * FOLD, FOLD), :] = total


def local(image_embed, text_embed, logit_scale, logit_bias):
    row_count, feature_count = text_embed.shape
    sizes = tuple(lax.axis_size(name) for name in MESH_AXES)
    groups = exchange_groups(sizes)
    places = len(groups[0])
    core = lax.axis_index("core")
    image_core = core == 0
    swap = [(0, 1), (1, 0)]

    def exchange(array):
        return lax.all_to_all(
            array, MESH_AXES, 0, 0, axis_index_groups=groups, tiled=True
        )

    def along_x(array):
        return lax.ppermute(array, ("x", "core"), x_pairs(lax.axis_size("x")))

    kept = jnp.where(image_core, image_embed, text_embed)
    arrived = lax.ppermute(jnp.where(image_core, text_embed, image_embed), "core", swap)
    chip = jnp.concatenate(
        [jnp.where(image_core, kept, arrived), jnp.where(image_core, arrived, kept)], axis=0
    )
    near = exchange(jnp.broadcast_to(chip[None], (places, *chip.shape)))
    near = near.reshape(-1, feature_count)
    far = along_x(near)
    other_near = lax.ppermute(near, "core", swap)
    other_far = lax.ppermute(far, "core", swap)

    numbers = jnp.concatenate([logit_scale, logit_bias])
    image_place, text_place = lax.axis_index(IMAGE_AXES), lax.axis_index(TEXT_AXES)
    place = jnp.where(
        image_core, jnp.stack([image_place, text_place]), jnp.stack([text_place, image_place])
    )
    smem = pl.BlockSpec(memory_space=pltpu.SMEM)
    vmem = pl.BlockSpec(memory_space=pltpu.VMEM)
    rows = near.shape[0]
    width = row_count // FOLD * feature_count + LANES

    def wide(*shape):
        return jax.ShapeDtypeStruct(shape, jnp.float32)

    def call(kernel, name, in_specs, out_shape, *arguments, blocks=0, scratch=()):
        return pl.pallas_call(
            kernel,
            out_shape=out_shape,
            in_specs=in_specs,
            out_specs=jax.tree.map(lambda _: vmem, out_shape),
            scratch_shapes=scratch,
            compiler_params=pltpu.CompilerParams(vmem_limit_bytes=20 * 2**20),
            cost_estimate=pl.CostEstimate(
                flops=4 * blocks * rows * rows * feature_count,
                bytes_accessed=8 * rows * feature_count,
                transcendentals=blocks * rows * rows,
            ),
            name=name,
        )(*arguments)

    total = wide(rows, feature_count)
    packed = wide(2 * places, FOLD, width)
    result = wide(row_count, feature_count)
    near_part = call(
        lambda *refs: near_kernel(2 * row_count, *refs), "near_near", [smem, smem, vmem, vmem],
        total, place, numbers, near, other_near, blocks=1,
    )
    far_packed = call(
        far_kernel, "far_rows", [smem, vmem, vmem, vmem], packed,
        numbers, far, other_near, other_far,
        blocks=2, scratch=[pltpu.VMEM(total.shape, jnp.float32)],
    )
    arrived = along_x(far_packed.astype(jnp.float16)).astype(jnp.float32)
    near_part = call(
        rest_kernel, "near_far", [smem, vmem, vmem, vmem], total,
        numbers, near, other_far, near_part, blocks=1,
    )
    near_packed = call(add_kernel, "add_x", [vmem, vmem], packed, near_part, arrived)
    sums = exchange(near_packed.astype(jnp.float16)).astype(jnp.float32)
    own, sent = call(
        sum_kernel, "sum_parts", [smem, vmem], (result, result), core[None], sums
    )
    sibling = lax.ppermute(sent, "core", swap)
    return (jnp.where(image_core, own, sibling), jnp.where(image_core, sibling, own))


def solution(mesh):
    rows = P(MESH_AXES, None)
    return jax.shard_map(
        local,
        mesh=finer_mesh(mesh),
        in_specs=(rows, rows, P(), P()),
        out_specs=(rows, rows),
        check_vma=False,
    )
```

```python
import jax
import jax.numpy as jnp
import numpy as np
from jax import lax
from jax.experimental import pallas as pl
from jax.experimental.pallas import tpu as pltpu
from jax.sharding import Mesh, PartitionSpec as P

MESH_AXES = ("z_hi", "x", "core", "y", "z_lo")
LOG2_E = 1.4426950408889634
LANES = 128
FOLD = 8


def finer_mesh(mesh):
    return Mesh(mesh.devices.reshape(4, 4, 2, 8, 2), MESH_AXES)


def exchange_groups(sizes):
    places = np.arange(np.prod(sizes)).reshape(sizes)
    x_count, y_count = sizes[1], sizes[3]
    groups = []
    for x in range(0, x_count, 2):
        pair = [x, x + 1]
        for y in range(y_count):
            groups.append(places[:, pair, 0, y, :].transpose(1, 0, 2).reshape(-1).tolist())
    for x in range(1, x_count, 2):
        pair = [x, (x + 1) % x_count]
        for z_hi in range(sizes[0]):
            for z_lo in range(sizes[4]):
                groups.append(places[z_hi, pair, 1, :, z_lo].reshape(-1).tolist())
    return groups


def weights_of(mine, other, scale_value, bias_value, same=None):
    products = lax.dot_general(
        mine, other, (((1,), (1,)), ((), ())), preferred_element_type=jnp.float32
    )
    exponent = products * (-LOG2_E * scale_value) + (-LOG2_E * bias_value)
    if same is None:
        return (scale_value / (1.0 + jnp.exp2(exponent))).astype(jnp.bfloat16)
    magnitude = scale_value / (1.0 + jnp.exp2(jnp.where(same, -exponent, exponent)))
    return jnp.where(same, -magnitude, magnitude).astype(jnp.bfloat16)


def pack_into(packed_ref, block, values):
    rows, width = values.shape
    largest = jnp.max(jnp.abs(values), axis=-1, keepdims=True)
    power = jnp.floor(jnp.log2(jnp.maximum(largest, 2.0**-100)))
    scaled = values * jnp.exp2(13.0 - power)
    lane = lax.broadcasted_iota(jnp.int32, (FOLD, LANES), 1)
    tail = jnp.zeros((FOLD, LANES), jnp.float32)
    for k in range(rows // FOLD):
        part = slice(k * FOLD, (k + 1) * FOLD)
        packed_ref[block, :, k * width : (k + 1) * width] = scaled[part, :]
        tail = jnp.where(lane == k, power[part, :], tail)
    packed_ref[block, :, rows // FOLD * width :] = tail


def block_kernel(chip_rows, place_ref, numbers_ref, mine_ref, other_ref, packed_ref, total_ref):
    rows = mine_ref.shape[0]
    scale_value, bias_value = numbers_ref[0], numbers_ref[1]
    other = other_ref[...]
    step = rows // 3
    for start in range(0, rows, step):
        part = pl.ds(start, step)
        weight = weights_of(mine_ref[part, :], other, scale_value, bias_value)
        total_ref[part, :] = jnp.dot(weight, other, preferred_element_type=jnp.float32)

    shape = (chip_rows, other.shape[0])
    band = pl.ds(pl.multiple_of(place_ref[0] * chip_rows, 16), chip_rows)
    row = lax.broadcasted_iota(jnp.int32, shape, 0)
    column = lax.broadcasted_iota(jnp.int32, shape, 1) - place_ref[1] * chip_rows
    weight = weights_of(mine_ref[band, :], other, scale_value, bias_value, row == column)
    total_ref[band, :] = jnp.dot(weight, other, preferred_element_type=jnp.float32)

    blocks = packed_ref.shape[0]
    block_rows = rows // blocks
    for block in range(blocks):
        pack_into(packed_ref, block, total_ref[pl.ds(block * block_rows, block_rows), :])


def sum_kernel(core_ref, packed_ref, own_ref, sent_ref):
    rows, width = own_ref.shape
    folds = rows // FOLD
    for out_ref, core in ((own_ref, core_ref[0]), (sent_ref, 1 - core_ref[0])):
        for k in range(folds):
            total = jnp.zeros((FOLD, width), jnp.float32)
            for place in range(packed_ref.shape[0] // 2):
                block = 2 * place + core
                factor = jnp.exp2(packed_ref[block, :, folds * width :] - 13.0)[:, k : k + 1]
                total = total + packed_ref[block, :, k * width : (k + 1) * width] * factor
            out_ref[pl.ds(k * FOLD, FOLD), :] = total


def local(image_embed, text_embed, logit_scale, logit_bias):
    row_count, feature_count = text_embed.shape
    sizes = tuple(lax.axis_size(name) for name in MESH_AXES)
    groups = exchange_groups(sizes)
    places = len(groups[0])
    core = lax.axis_index("core")
    image_core = core == 0
    swap = [(0, 1), (1, 0)]

    def exchange(array):
        return lax.all_to_all(
            array, MESH_AXES, 0, 0, axis_index_groups=groups, tiled=True
        )

    kept = jnp.where(image_core, image_embed, text_embed)
    arrived = lax.ppermute(jnp.where(image_core, text_embed, image_embed), "core", swap)
    chip = jnp.concatenate(
        [jnp.where(image_core, kept, arrived), jnp.where(image_core, arrived, kept)], axis=0
    )
    mine = exchange(jnp.broadcast_to(chip[None], (places, *chip.shape)))
    mine = mine.reshape(-1, feature_count)
    other = lax.ppermute(mine, "core", swap)

    numbers = jnp.concatenate([logit_scale, logit_bias])
    x, y = lax.axis_index("x"), lax.axis_index("y")
    z_count = sizes[0] * sizes[4]
    image_place = x % 2 * z_count + lax.axis_index(("z_hi", "z_lo"))
    text_place = (x + 1) % 2 * sizes[3] + y
    place = jnp.where(
        image_core, jnp.stack([image_place, text_place]), jnp.stack([text_place, image_place])
    )
    smem = pl.BlockSpec(memory_space=pltpu.SMEM)
    vmem = pl.BlockSpec(memory_space=pltpu.VMEM)
    params = pltpu.CompilerParams(vmem_limit_bytes=24 * 2**20)
    rows = mine.shape[0]
    width = row_count // FOLD * feature_count + LANES
    packed = pl.pallas_call(
        lambda *refs: block_kernel(2 * row_count, *refs),
        out_shape=jax.ShapeDtypeStruct((2 * places, FOLD, width), jnp.float32),
        in_specs=[smem, smem, vmem, vmem],
        out_specs=vmem,
        scratch_shapes=[pltpu.VMEM((rows, feature_count), jnp.float32)],
        compiler_params=params,
        cost_estimate=pl.CostEstimate(
            flops=4 * rows * rows * feature_count,
            bytes_accessed=8 * rows * feature_count,
            transcendentals=rows * rows,
        ),
        name="block",
    )(place, numbers, mine, other)
    sums = exchange(packed.astype(jnp.float16)).astype(jnp.float32)
    result = jax.ShapeDtypeStruct((row_count, feature_count), jnp.float32)
    own, sent = pl.pallas_call(
        sum_kernel,
        out_shape=(result, result),
        in_specs=[smem, vmem],
        out_specs=(vmem, vmem),
        compiler_params=params,
        cost_estimate=pl.CostEstimate(
            flops=4 * rows * feature_count,
            bytes_accessed=4 * rows * feature_count,
            transcendentals=0,
        ),
        name="sum_parts",
    )(core[None], sums)
    sibling = lax.ppermute(sent, "core", swap)
    return (jnp.where(image_core, own, sibling), jnp.where(image_core, sibling, own))


def solution(mesh):
    rows = P(MESH_AXES, None)
    return jax.shard_map(
        local,
        mesh=finer_mesh(mesh),
        in_specs=(rows, rows, P(), P()),
        out_specs=(rows, rows),
        check_vma=False,
    )
```

```python
import jax
import jax.numpy as jnp
import numpy as np
from jax import lax
from jax.experimental import pallas as pl
from jax.experimental.pallas import tpu as pltpu
from jax.sharding import Mesh, PartitionSpec as P

MESH_AXES = ("z_hi", "x", "core", "y", "z_lo")
LOG2_E = 1.4426950408889634
LANES = 128
FOLD = 8


def finer_mesh(mesh):
    return Mesh(mesh.devices.reshape(4, 4, 2, 8, 2), MESH_AXES)


def exchange_groups(sizes):
    places = np.arange(np.prod(sizes)).reshape(sizes)
    x_count, y_count = sizes[1], sizes[3]
    groups = []
    for x in range(0, x_count, 2):
        pair = [x, x + 1]
        for y in range(y_count):
            groups.append(places[:, pair, 0, y, :].transpose(1, 0, 2).reshape(-1).tolist())
    for x in range(1, x_count, 2):
        pair = [x, (x + 1) % x_count]
        for z_hi in range(sizes[0]):
            for z_lo in range(sizes[4]):
                groups.append(places[z_hi, pair, 1, :, z_lo].reshape(-1).tolist())
    return groups


def x_pairs(count):
    pairs = []
    for x in range(count):
        for core in range(2):
            step = 1 if (x + core) % 2 == 0 else -1
            pairs.append((2 * x + core, 2 * ((x + step) % count) + core))
    return pairs


def ring(sizes, step):
    places = np.arange(np.prod(sizes)).reshape(sizes)
    along_z = places[:, :, 0].transpose(0, 3, 1, 2).reshape(-1, sizes[1] * sizes[3])
    along_y = places[:, :, 1].transpose(2, 0, 1, 3)
    pairs = []
    for array in (along_z, along_y):
        pairs += zip(array.reshape(-1).tolist(), np.roll(array, -step, 0).reshape(-1).tolist())
    return pairs


def weights_of(mine, other, scale_value, bias_value, paired=0):
    products = lax.dot_general(
        mine, other, (((1,), (1,)), ((), ())), preferred_element_type=jnp.float32
    )
    exponent = products * (-LOG2_E * scale_value) + (-LOG2_E * bias_value)
    if not paired:
        return (scale_value / (1.0 + jnp.exp2(exponent))).astype(jnp.bfloat16)
    count = min(LANES, exponent.shape[1])
    first = exponent[:, :count]
    row = lax.broadcasted_iota(jnp.int32, first.shape, 0)
    same = (row == lax.broadcasted_iota(jnp.int32, first.shape, 1)) & (row < paired)
    magnitude = scale_value / (1.0 + jnp.exp2(jnp.where(same, -first, first)))
    weight = jnp.where(same, -magnitude, magnitude)
    if count < exponent.shape[1]:
        rest = scale_value / (1.0 + jnp.exp2(exponent[:, count:]))
        weight = jnp.concatenate([weight, rest], axis=1)
    return weight.astype(jnp.bfloat16)


def pack_into(packed_ref, block, values):
    rows, width = values.shape
    largest = jnp.max(jnp.abs(values), axis=-1, keepdims=True)
    power = jnp.floor(jnp.log2(jnp.maximum(largest, 2.0**-100)))
    scaled = values * jnp.exp2(13.0 - power)
    lane = lax.broadcasted_iota(jnp.int32, (FOLD, LANES), 1)
    tail = jnp.zeros((FOLD, LANES), jnp.float32)
    for k in range(rows // FOLD):
        part = slice(k * FOLD, (k + 1) * FOLD)
        packed_ref[block, :, k * width : (k + 1) * width] = scaled[part, :]
        tail = jnp.where(lane == k, power[part, :], tail)
    packed_ref[block, :, rows // FOLD * width :] = tail


def block_kernel(
    offsets,
    chip_rows,
    place_ref,
    numbers_ref,
    mine_first_ref,
    mine_last_ref,
    other_first_ref,
    other_last_ref,
    packed_ref,
    other_ref,
    total_ref,
):
    scale_value, bias_value = numbers_ref[0], numbers_ref[1]
    split, rows = mine_first_ref.shape[0], other_ref.shape[0]
    other_ref[pl.ds(0, split), :] = other_first_ref[...]
    other_ref[pl.ds(split, rows - split), :] = other_last_ref[...]
    other = other_ref[...]
    half = split // 2
    for start, mine, paired in (
        (0, mine_first_ref[pl.ds(0, half), :], chip_rows),
        (half, mine_first_ref[pl.ds(half, half), :], 0),
        (split, mine_last_ref[...], 0),
    ):
        weight = weights_of(mine, other, scale_value, bias_value, paired)
        total_ref[pl.ds(start, mine.shape[0]), :] = jnp.dot(
            weight, other, preferred_element_type=jnp.float32
        )

    places = packed_ref.shape[0] // 2
    length = places // 2
    block_rows = chip_rows // 2
    for at, (pair, offset) in enumerate(offsets):
        across = lax.rem(place_ref[0] + pair, 2)
        along = lax.rem(place_ref[1] + (offset + length), length)
        for core in range(2):
            block = 2 * (across * length + along) + core
            part = pl.ds((2 * at + core) * block_rows, block_rows)
            pack_into(packed_ref, block, total_ref[part, :])


def sum_kernel(core_ref, packed_ref, own_ref, sent_ref):
    rows, width = own_ref.shape
    folds = rows // FOLD
    for out_ref, core in ((own_ref, core_ref[0]), (sent_ref, 1 - core_ref[0])):
        for k in range(folds):
            total = jnp.zeros((FOLD, width), jnp.float32)
            for place in range(packed_ref.shape[0] // 2):
                block = 2 * place + core
                factor = jnp.exp2(packed_ref[block, :, folds * width :] - 13.0)[:, k : k + 1]
                total = total + packed_ref[block, :, k * width : (k + 1) * width] * factor
            out_ref[pl.ds(k * FOLD, FOLD), :] = total


def local(image_embed, text_embed, logit_scale, logit_bias):
    row_count, feature_count = text_embed.shape
    sizes = tuple(lax.axis_size(name) for name in MESH_AXES)
    groups = exchange_groups(sizes)
    places = len(groups[0])
    core = lax.axis_index("core")
    image_core = core == 0
    swap = [(0, 1), (1, 0)]

    def exchange(array):
        return lax.all_to_all(
            array, MESH_AXES, 0, 0, axis_index_groups=groups, tiled=True
        )

    kept = jnp.where(image_core, image_embed, text_embed)
    arrived = lax.ppermute(jnp.where(image_core, text_embed, image_embed), "core", swap)
    chip = jnp.concatenate(
        [jnp.where(image_core, kept, arrived), jnp.where(image_core, arrived, kept)], axis=0
    )
    beside = lax.ppermute(chip, ("x", "core"), x_pairs(sizes[1]))
    column = jnp.concatenate([chip, beside], axis=0)
    length = places // 2
    up = down = column
    pieces, offsets = [column], [(0, 0), (1, 0)]
    for k in range(1, length // 2):
        up = lax.ppermute(up, MESH_AXES, ring(sizes, 1))
        down = lax.ppermute(down, MESH_AXES, ring(sizes, -1))
        pieces += [up, down]
        offsets += [(0, -k), (1, -k), (0, k), (1, k)]
    chip_rows = 2 * row_count
    pieces.append(lax.ppermute(up[:chip_rows], MESH_AXES, ring(sizes, 1)))
    pieces.append(lax.ppermute(down[chip_rows:], MESH_AXES, ring(sizes, -1)))
    offsets += [(0, length // 2), (1, length // 2)]
    cut = max(1, len(pieces) - 4)
    mine_first = jnp.concatenate(pieces[:cut], axis=0)
    mine_last = jnp.concatenate(pieces[cut:], axis=0)
    other_first = lax.ppermute(mine_first, "core", swap)
    other_last = lax.ppermute(mine_last, "core", swap)

    numbers = jnp.concatenate([logit_scale, logit_bias])
    across = (lax.axis_index("x") + core) % 2
    along = jnp.where(image_core, lax.axis_index(("z_hi", "z_lo")), lax.axis_index("y"))
    place = jnp.stack([across, along])
    smem = pl.BlockSpec(memory_space=pltpu.SMEM)
    vmem = pl.BlockSpec(memory_space=pltpu.VMEM)
    params = pltpu.CompilerParams(vmem_limit_bytes=24 * 2**20)
    rows = chip_rows * places
    width = row_count // FOLD * feature_count + LANES
    packed = pl.pallas_call(
        lambda *refs: block_kernel(offsets, chip_rows, *refs),
        out_shape=jax.ShapeDtypeStruct((2 * places, FOLD, width), jnp.float32),
        in_specs=[smem, smem, vmem, vmem, vmem, vmem],
        out_specs=vmem,
        scratch_shapes=[
            pltpu.VMEM((rows, feature_count), jnp.bfloat16),
            pltpu.VMEM((rows, feature_count), jnp.float32),
        ],
        compiler_params=params,
        cost_estimate=pl.CostEstimate(
            flops=4 * rows * rows * feature_count,
            bytes_accessed=8 * rows * feature_count,
            transcendentals=rows * rows,
        ),
        name="block",
    )(place, numbers, mine_first, mine_last, other_first, other_last)
    sums = exchange(packed.astype(jnp.float16)).astype(jnp.float32)
    result = jax.ShapeDtypeStruct((row_count, feature_count), jnp.float32)
    own, sent = pl.pallas_call(
        sum_kernel,
        out_shape=(result, result),
        in_specs=[smem, vmem],
        out_specs=(vmem, vmem),
        compiler_params=params,
        cost_estimate=pl.CostEstimate(
            flops=4 * rows * feature_count,
            bytes_accessed=4 * rows * feature_count,
            transcendentals=0,
        ),
        name="sum_parts",
    )(core[None], sums)
    sibling = lax.ppermute(sent, "core", swap)
    return (jnp.where(image_core, own, sibling), jnp.where(image_core, sibling, own))


def solution(mesh):
    rows = P(MESH_AXES, None)
    return jax.shard_map(
        local,
        mesh=finer_mesh(mesh),
        in_specs=(rows, rows, P(), P()),
        out_specs=(rows, rows),
        check_vma=False,
    )
```

```python
import jax
import jax.numpy as jnp
import numpy as np
from jax import lax
from jax.experimental import pallas as pl
from jax.experimental.pallas import tpu as pltpu
from jax.sharding import Mesh, PartitionSpec as P

MESH_AXES = ("z_hi", "x", "core", "y", "z_lo")
LOG2_E = 1.4426950408889634
LANES = 128
FOLD = 8


def finer_mesh(mesh):
    return Mesh(mesh.devices.reshape(4, 4, 2, 8, 2), MESH_AXES)


def exchange_groups(sizes):
    places = np.arange(np.prod(sizes)).reshape(sizes)
    x_count, y_count = sizes[1], sizes[3]
    groups = []
    for x in range(0, x_count, 2):
        pair = [x, x + 1]
        for y in range(y_count):
            groups.append(places[:, pair, 0, y, :].transpose(1, 0, 2).reshape(-1).tolist())
    for x in range(1, x_count, 2):
        pair = [x, (x + 1) % x_count]
        for z_hi in range(sizes[0]):
            for z_lo in range(sizes[4]):
                groups.append(places[z_hi, pair, 1, :, z_lo].reshape(-1).tolist())
    return groups


def products_of(mine, other):
    return lax.dot_general(
        mine, other, (((1,), (1,)), ((), ())), preferred_element_type=jnp.float32
    )


def weights_of(products, scale_value, bias_value, pair):
    same = lax.broadcasted_iota(jnp.int32, products.shape, 1) == pair
    exponent = products * (-LOG2_E * scale_value) + (-LOG2_E * bias_value)
    magnitude = scale_value / (1.0 + jnp.exp2(jnp.where(same, -exponent, exponent)))
    return jnp.where(same, -magnitude, magnitude).astype(jnp.bfloat16)


def pack_into(packed_ref, block, values):
    rows, width = values.shape
    largest = jnp.max(jnp.abs(values), axis=-1, keepdims=True)
    power = jnp.floor(jnp.log2(jnp.maximum(largest, 2.0**-100)))
    scaled = values * jnp.exp2(13.0 - power)
    lane = lax.broadcasted_iota(jnp.int32, (FOLD, LANES), 1)
    tail = jnp.zeros((FOLD, LANES), jnp.float32)
    for k in range(rows // FOLD):
        part = slice(k * FOLD, (k + 1) * FOLD)
        packed_ref[block, :, k * width : (k + 1) * width] = scaled[part, :]
        tail = jnp.where(lane == k, power[part, :], tail)
    packed_ref[block, :, rows // FOLD * width :] = tail


def block_kernel(place_ref, numbers_ref, mine_ref, other_ref, packed_ref, total_ref):
    rows = mine_ref.shape[0]
    scale_value, bias_value = numbers_ref[0], numbers_ref[1]
    places = packed_ref.shape[0]
    chip_rows = rows // places
    other = other_ref[...]
    step = rows // 2
    halves = (0, step)
    products = [products_of(mine_ref[pl.ds(start, step), :], other) for start in halves]
    for start, product in zip(halves, products):
        row = lax.broadcasted_iota(jnp.int32, (step, 1), 0) + start - place_ref[0] * chip_rows
        own = (row >= 0) & (row < chip_rows)
        pair = jnp.where(own, row + place_ref[1] * chip_rows, -1)
        weight = weights_of(product, scale_value, bias_value, pair)
        total_ref[pl.ds(start, step), :] = jnp.dot(
            weight, other, preferred_element_type=jnp.float32
        )
    for place in range(places):
        pack_into(packed_ref, place, total_ref[pl.ds(place * chip_rows, chip_rows), :])


def sum_kernel(core_ref, packed_ref, own_ref, sent_ref):
    rows, width = own_ref.shape
    folds = rows // FOLD
    totals = []
    for k in range(2 * folds):
        total = jnp.zeros((FOLD, width), jnp.float32)
        for place in range(packed_ref.shape[0]):
            factor = jnp.exp2(packed_ref[place, :, 2 * folds * width :] - 13.0)[:, k : k + 1]
            total = total + packed_ref[place, :, k * width : (k + 1) * width] * factor
        totals.append(total)
    first = core_ref[0] == 0
    for k in range(folds):
        part = pl.ds(k * FOLD, FOLD)
        own_ref[part, :] = jnp.where(first, totals[k], totals[folds + k])
        sent_ref[part, :] = jnp.where(first, totals[folds + k], totals[k])


def local(image_embed, text_embed, logit_scale, logit_bias):
    row_count, feature_count = text_embed.shape
    sizes = tuple(lax.axis_size(name) for name in MESH_AXES)
    groups = exchange_groups(sizes)
    places = len(groups[0])
    core = lax.axis_index("core")
    image_core = core == 0
    swap = [(0, 1), (1, 0)]

    def exchange(array):
        return lax.all_to_all(
            array, MESH_AXES, 0, 0, axis_index_groups=groups, tiled=True
        )

    kept = jnp.where(image_core, image_embed, text_embed)
    arrived = lax.ppermute(jnp.where(image_core, text_embed, image_embed), "core", swap)
    chip = jnp.concatenate(
        [jnp.where(image_core, kept, arrived), jnp.where(image_core, arrived, kept)], axis=0
    )
    mine = exchange(jnp.broadcast_to(chip[None], (places, *chip.shape)))
    mine = mine.reshape(-1, feature_count)
    other = lax.ppermute(mine, "core", swap)

    numbers = jnp.concatenate([logit_scale, logit_bias])
    x, y = lax.axis_index("x"), lax.axis_index("y")
    z_count = sizes[0] * sizes[4]
    image_place = x % 2 * z_count + lax.axis_index(("z_hi", "z_lo"))
    text_place = (x + 1) % 2 * sizes[3] + y
    place = jnp.where(
        image_core, jnp.stack([image_place, text_place]), jnp.stack([text_place, image_place])
    )
    smem = pl.BlockSpec(memory_space=pltpu.SMEM)
    vmem = pl.BlockSpec(memory_space=pltpu.VMEM)
    params = pltpu.CompilerParams(vmem_limit_bytes=24 * 2**20)
    rows = mine.shape[0]
    width = 2 * row_count // FOLD * feature_count + LANES
    packed = pl.pallas_call(
        block_kernel,
        out_shape=jax.ShapeDtypeStruct((places, FOLD, width), jnp.float32),
        in_specs=[smem, smem, vmem, vmem],
        out_specs=vmem,
        scratch_shapes=[pltpu.VMEM((rows, feature_count), jnp.float32)],
        compiler_params=params,
        cost_estimate=pl.CostEstimate(
            flops=4 * rows * rows * feature_count,
            bytes_accessed=8 * rows * feature_count,
            transcendentals=rows * rows,
        ),
        name="block",
    )(place, numbers, mine, other)
    sums = exchange(packed.astype(jnp.float16)).astype(jnp.float32)
    result = jax.ShapeDtypeStruct((row_count, feature_count), jnp.float32)
    own, sent = pl.pallas_call(
        sum_kernel,
        out_shape=(result, result),
        in_specs=[smem, vmem],
        out_specs=(vmem, vmem),
        compiler_params=params,
        cost_estimate=pl.CostEstimate(
            flops=4 * rows * feature_count,
            bytes_accessed=4 * rows * feature_count,
            transcendentals=0,
        ),
        name="sum_parts",
    )(core[None], sums)
    sibling = lax.ppermute(sent, "core", swap)
    return (jnp.where(image_core, own, sibling), jnp.where(image_core, sibling, own))


def solution(mesh):
    rows = P(MESH_AXES, None)
    return jax.shard_map(
        local,
        mesh=finer_mesh(mesh),
        in_specs=(rows, rows, P(), P()),
        out_specs=(rows, rows),
        check_vma=False,
    )
```

```python
import jax
import jax.numpy as jnp
import numpy as np
from jax import lax
from jax.experimental import pallas as pl
from jax.experimental.pallas import tpu as pltpu
from jax.sharding import Mesh, PartitionSpec as P

MESH_AXES = ("z_hi", "x", "core", "y", "z_lo")
LOG2_E = 1.4426950408889634
LANES = 128
FOLD = 8


def finer_mesh(mesh):
    return Mesh(mesh.devices.reshape(4, 4, 2, 8, 2), MESH_AXES)


def reversed_bits(value, count):
    bits = count.bit_length() - 1
    return sum(((value >> i) & 1) << (bits - 1 - i) for i in range(bits))


def exchange_groups(sizes):
    places = np.arange(np.prod(sizes)).reshape(sizes)
    x_count = sizes[1]
    along_z = places[:, :, 0].transpose(0, 3, 1, 2).reshape(-1, x_count, sizes[3])
    along_y = places[:, :, 1].transpose(2, 1, 0, 3).reshape(sizes[3], x_count, -1)
    groups = []
    for first, array in ((0, along_z), (1, along_y)):
        length = array.shape[0]
        array = array[[reversed_bits(i, length) for i in range(length)]]
        for x in range(first, x_count, 2):
            for other in range(array.shape[2]):
                groups.append(array[:, [x, (x + 1) % x_count], other].reshape(-1).tolist())
    return groups


def products_of(mine, other):
    return lax.dot_general(
        mine, other, (((1,), (1,)), ((), ())), preferred_element_type=jnp.float32
    )


def weights_of(products, scale_value, bias_value, pair):
    same = lax.broadcasted_iota(jnp.int32, products.shape, 1) == pair
    exponent = products * (-LOG2_E * scale_value) + (-LOG2_E * bias_value)
    magnitude = scale_value / (1.0 + jnp.exp2(jnp.where(same, -exponent, exponent)))
    return jnp.where(same, -magnitude, magnitude).astype(jnp.bfloat16)


def pack_into(packed_ref, block, values):
    rows, width = values.shape
    largest = jnp.max(jnp.abs(values), axis=-1, keepdims=True)
    power = jnp.floor(jnp.log2(jnp.maximum(largest, 2.0**-100)))
    scaled = values * jnp.exp2(13.0 - power)
    lane = lax.broadcasted_iota(jnp.int32, (FOLD, LANES), 1)
    tail = jnp.zeros((FOLD, LANES), jnp.float32)
    for k in range(rows // FOLD):
        part = slice(k * FOLD, (k + 1) * FOLD)
        packed_ref[block, :, k * width : (k + 1) * width] = scaled[part, :]
        tail = jnp.where(lane == k, power[part, :], tail)
    packed_ref[block, :, rows // FOLD * width :] = tail


def block_kernel(place_ref, numbers_ref, mine_ref, other_ref, packed_ref, total_ref):
    rows = mine_ref.shape[0]
    scale_value, bias_value = numbers_ref[0], numbers_ref[1]
    places = packed_ref.shape[0]
    chip_rows = rows // places
    other = other_ref[...]
    step = rows // 2
    halves = (0, step)
    products = [products_of(mine_ref[pl.ds(start, step), :], other) for start in halves]
    for start, product in zip(halves, products):
        row = lax.broadcasted_iota(jnp.int32, (step, 1), 0) + start - place_ref[0] * chip_rows
        own = (row >= 0) & (row < chip_rows)
        pair = jnp.where(own, row + place_ref[1] * chip_rows, -1)
        weight = weights_of(product, scale_value, bias_value, pair)
        total_ref[pl.ds(start, step), :] = jnp.dot(
            weight, other, preferred_element_type=jnp.float32
        )
    for place in range(places):
        pack_into(packed_ref, place, total_ref[pl.ds(place * chip_rows, chip_rows), :])


def sum_kernel(core_ref, packed_ref, own_ref, sent_ref):
    rows, width = own_ref.shape
    folds = rows // FOLD
    totals = []
    for k in range(2 * folds):
        total = jnp.zeros((FOLD, width), jnp.float32)
        for place in range(packed_ref.shape[0]):
            factor = jnp.exp2(packed_ref[place, :, 2 * folds * width :] - 13.0)[:, k : k + 1]
            total = total + packed_ref[place, :, k * width : (k + 1) * width] * factor
        totals.append(total)
    first = core_ref[0] == 0
    for k in range(folds):
        part = pl.ds(k * FOLD, FOLD)
        own_ref[part, :] = jnp.where(first, totals[k], totals[folds + k])
        sent_ref[part, :] = jnp.where(first, totals[folds + k], totals[k])


def local(image_embed, text_embed, logit_scale, logit_bias):
    row_count, feature_count = text_embed.shape
    sizes = tuple(lax.axis_size(name) for name in MESH_AXES)
    groups = exchange_groups(sizes)
    places = len(groups[0])
    core = lax.axis_index("core")
    image_core = core == 0
    swap = [(0, 1), (1, 0)]

    def exchange(array):
        return lax.all_to_all(
            array, MESH_AXES, 0, 0, axis_index_groups=groups, tiled=True
        )

    kept = jnp.where(image_core, image_embed, text_embed)
    arrived = lax.ppermute(jnp.where(image_core, text_embed, image_embed), "core", swap)
    chip = jnp.concatenate(
        [jnp.where(image_core, kept, arrived), jnp.where(image_core, arrived, kept)], axis=0
    )
    mine = exchange(jnp.broadcast_to(chip[None], (places, *chip.shape)))
    mine = mine.reshape(-1, feature_count)
    other = lax.ppermute(mine, "core", swap)

    numbers = jnp.concatenate([logit_scale, logit_bias])
    x, y = lax.axis_index("x"), lax.axis_index("y")
    z_count = sizes[0] * sizes[4]
    z = lax.axis_index(("z_hi", "z_lo"))
    image_place = reversed_bits(z, z_count) * 2 + x % 2
    text_place = reversed_bits(y, sizes[3]) * 2 + (x + 1) % 2
    place = jnp.where(
        image_core, jnp.stack([image_place, text_place]), jnp.stack([text_place, image_place])
    )
    smem = pl.BlockSpec(memory_space=pltpu.SMEM)
    vmem = pl.BlockSpec(memory_space=pltpu.VMEM)
    params = pltpu.CompilerParams(vmem_limit_bytes=24 * 2**20)
    rows = mine.shape[0]
    width = 2 * row_count // FOLD * feature_count + LANES
    packed = pl.pallas_call(
        block_kernel,
        out_shape=jax.ShapeDtypeStruct((places, FOLD, width), jnp.float32),
        in_specs=[smem, smem, vmem, vmem],
        out_specs=vmem,
        scratch_shapes=[pltpu.VMEM((rows, feature_count), jnp.float32)],
        compiler_params=params,
        cost_estimate=pl.CostEstimate(
            flops=4 * rows * rows * feature_count,
            bytes_accessed=8 * rows * feature_count,
            transcendentals=rows * rows,
        ),
        name="block",
    )(place, numbers, mine, other)
    sums = exchange(packed.astype(jnp.float16)).astype(jnp.float32)
    result = jax.ShapeDtypeStruct((row_count, feature_count), jnp.float32)
    own, sent = pl.pallas_call(
        sum_kernel,
        out_shape=(result, result),
        in_specs=[smem, vmem],
        out_specs=(vmem, vmem),
        compiler_params=params,
        cost_estimate=pl.CostEstimate(
            flops=4 * rows * feature_count,
            bytes_accessed=4 * rows * feature_count,
            transcendentals=0,
        ),
        name="sum_parts",
    )(core[None], sums)
    sibling = lax.ppermute(sent, "core", swap)
    return (jnp.where(image_core, own, sibling), jnp.where(image_core, sibling, own))


def solution(mesh):
    rows = P(MESH_AXES, None)
    return jax.shard_map(
        local,
        mesh=finer_mesh(mesh),
        in_specs=(rows, rows, P(), P()),
        out_specs=(rows, rows),
        check_vma=False,
    )
```

```python
import jax
import jax.numpy as jnp
import numpy as np
from jax import lax
from jax.experimental import pallas as pl
from jax.experimental.pallas import tpu as pltpu
from jax.sharding import Mesh, PartitionSpec as P

MESH_AXES = ("z_hi", "x", "core", "y", "z_lo")
LOG2_E = 1.4426950408889634
LANES = 128
FOLD = 8
STRIDE = 3


def finer_mesh(mesh):
    return Mesh(mesh.devices.reshape(4, 4, 2, 8, 2), MESH_AXES)


def exchange_groups(sizes):
    places = np.arange(np.prod(sizes)).reshape(sizes)
    x_count = sizes[1]
    along_z = places[:, :, 0].transpose(0, 3, 1, 2).reshape(-1, x_count, sizes[3])
    along_y = places[:, :, 1].transpose(2, 1, 0, 3).reshape(sizes[3], x_count, -1)
    groups = []
    for first, array in ((0, along_z), (1, along_y)):
        length = array.shape[0]
        array = array[[STRIDE * i % length for i in range(length)]]
        for x in range(first, x_count, 2):
            for other in range(array.shape[2]):
                groups.append(array[:, [x, (x + 1) % x_count], other].T.reshape(-1).tolist())
    return groups


def products_of(mine, other):
    return lax.dot_general(
        mine, other, (((1,), (1,)), ((), ())), preferred_element_type=jnp.float32
    )


def weights_of(products, scale_value, bias_value, pair):
    same = lax.broadcasted_iota(jnp.int32, products.shape, 1) == pair
    exponent = products * (-LOG2_E * scale_value) + (-LOG2_E * bias_value)
    magnitude = scale_value / (1.0 + jnp.exp2(jnp.where(same, -exponent, exponent)))
    return jnp.where(same, -magnitude, magnitude).astype(jnp.bfloat16)


def pack_into(packed_ref, block, values):
    rows, width = values.shape
    largest = jnp.max(jnp.abs(values), axis=-1, keepdims=True)
    power = jnp.floor(jnp.log2(jnp.maximum(largest, 2.0**-100)))
    scaled = values * jnp.exp2(13.0 - power)
    lane = lax.broadcasted_iota(jnp.int32, (FOLD, LANES), 1)
    tail = jnp.zeros((FOLD, LANES), jnp.float32)
    for k in range(rows // FOLD):
        part = slice(k * FOLD, (k + 1) * FOLD)
        packed_ref[block, :, k * width : (k + 1) * width] = scaled[part, :]
        tail = jnp.where(lane == k, power[part, :], tail)
    packed_ref[block, :, rows // FOLD * width :] = tail


def block_kernel(place_ref, numbers_ref, mine_ref, other_ref, packed_ref, total_ref):
    rows = mine_ref.shape[0]
    scale_value, bias_value = numbers_ref[0], numbers_ref[1]
    places = packed_ref.shape[0]
    chip_rows = rows // places
    other = other_ref[...]
    step = rows // 2
    halves = (0, step)
    products = [products_of(mine_ref[pl.ds(start, step), :], other) for start in halves]
    for start, product in zip(halves, products):
        row = lax.broadcasted_iota(jnp.int32, (step, 1), 0) + start - place_ref[0] * chip_rows
        own = (row >= 0) & (row < chip_rows)
        pair = jnp.where(own, row + place_ref[1] * chip_rows, -1)
        weight = weights_of(product, scale_value, bias_value, pair)
        total_ref[pl.ds(start, step), :] = jnp.dot(
            weight, other, preferred_element_type=jnp.float32
        )
    for place in range(places):
        pack_into(packed_ref, place, total_ref[pl.ds(place * chip_rows, chip_rows), :])


def sum_kernel(core_ref, packed_ref, own_ref, sent_ref):
    rows, width = own_ref.shape
    folds = rows // FOLD
    totals = []
    for k in range(2 * folds):
        total = jnp.zeros((FOLD, width), jnp.float32)
        for place in range(packed_ref.shape[0]):
            factor = jnp.exp2(packed_ref[place, :, 2 * folds * width :] - 13.0)[:, k : k + 1]
            total = total + packed_ref[place, :, k * width : (k + 1) * width] * factor
        totals.append(total)
    first = core_ref[0] == 0
    for k in range(folds):
        part = pl.ds(k * FOLD, FOLD)
        own_ref[part, :] = jnp.where(first, totals[k], totals[folds + k])
        sent_ref[part, :] = jnp.where(first, totals[folds + k], totals[k])


def local(image_embed, text_embed, logit_scale, logit_bias):
    row_count, feature_count = text_embed.shape
    sizes = tuple(lax.axis_size(name) for name in MESH_AXES)
    groups = exchange_groups(sizes)
    places = len(groups[0])
    core = lax.axis_index("core")
    image_core = core == 0
    swap = [(0, 1), (1, 0)]

    def exchange(array):
        return lax.all_to_all(
            array, MESH_AXES, 0, 0, axis_index_groups=groups, tiled=True
        )

    kept = jnp.where(image_core, image_embed, text_embed)
    arrived = lax.ppermute(jnp.where(image_core, text_embed, image_embed), "core", swap)
    chip = jnp.concatenate(
        [jnp.where(image_core, kept, arrived), jnp.where(image_core, arrived, kept)], axis=0
    )
    mine = exchange(jnp.broadcast_to(chip[None], (places, *chip.shape)))
    mine = mine.reshape(-1, feature_count)
    other = lax.ppermute(mine, "core", swap)

    numbers = jnp.concatenate([logit_scale, logit_bias])
    x, y = lax.axis_index("x"), lax.axis_index("y")
    z_count = sizes[0] * sizes[4]
    z = lax.axis_index(("z_hi", "z_lo"))
    image_place = x % 2 * z_count + STRIDE * z % z_count
    text_place = (x + 1) % 2 * sizes[3] + STRIDE * y % sizes[3]
    place = jnp.where(
        image_core, jnp.stack([image_place, text_place]), jnp.stack([text_place, image_place])
    )
    smem = pl.BlockSpec(memory_space=pltpu.SMEM)
    vmem = pl.BlockSpec(memory_space=pltpu.VMEM)
    params = pltpu.CompilerParams(vmem_limit_bytes=24 * 2**20)
    rows = mine.shape[0]
    width = 2 * row_count // FOLD * feature_count + LANES
    packed = pl.pallas_call(
        block_kernel,
        out_shape=jax.ShapeDtypeStruct((places, FOLD, width), jnp.float32),
        in_specs=[smem, smem, vmem, vmem],
        out_specs=vmem,
        scratch_shapes=[pltpu.VMEM((rows, feature_count), jnp.float32)],
        compiler_params=params,
        cost_estimate=pl.CostEstimate(
            flops=4 * rows * rows * feature_count,
            bytes_accessed=8 * rows * feature_count,
            transcendentals=rows * rows,
        ),
        name="block",
    )(place, numbers, mine, other)
    sums = exchange(packed.astype(jnp.float16)).astype(jnp.float32)
    result = jax.ShapeDtypeStruct((row_count, feature_count), jnp.float32)
    own, sent = pl.pallas_call(
        sum_kernel,
        out_shape=(result, result),
        in_specs=[smem, vmem],
        out_specs=(vmem, vmem),
        compiler_params=params,
        cost_estimate=pl.CostEstimate(
            flops=4 * rows * feature_count,
            bytes_accessed=4 * rows * feature_count,
            transcendentals=0,
        ),
        name="sum_parts",
    )(core[None], sums)
    sibling = lax.ppermute(sent, "core", swap)
    return (jnp.where(image_core, own, sibling), jnp.where(image_core, sibling, own))


def solution(mesh):
    rows = P(MESH_AXES, None)
    return jax.shard_map(
        local,
        mesh=finer_mesh(mesh),
        in_specs=(rows, rows, P(), P()),
        out_specs=(rows, rows),
        check_vma=False,
    )
```

```python
import jax
import jax.numpy as jnp
import numpy as np
from jax import lax
from jax.experimental import pallas as pl
from jax.experimental.pallas import tpu as pltpu
from jax.sharding import Mesh, PartitionSpec as P

MESH_AXES = ("z_hi", "x", "core", "y", "z_lo")
LOG2_E = 1.4426950408889634
LANES = 128
FOLD = 8


def finer_mesh(mesh):
    return Mesh(mesh.devices.reshape(4, 4, 2, 8, 2), MESH_AXES)


def exchange_groups(sizes):
    places = np.arange(np.prod(sizes)).reshape(sizes)
    x_count, y_count = sizes[1], sizes[3]
    groups = []
    for x in range(0, x_count, 2):
        pair = [x, x + 1]
        for y in range(y_count):
            groups.append(places[:, pair, 0, y, :].transpose(1, 0, 2).reshape(-1).tolist())
    for x in range(1, x_count, 2):
        pair = [x, (x + 1) % x_count]
        for z_hi in range(sizes[0]):
            for z_lo in range(sizes[4]):
                groups.append(places[z_hi, pair, 1, :, z_lo].reshape(-1).tolist())
    return groups


def products_of(mine, other):
    return lax.dot_general(
        mine, other, (((1,), (1,)), ((), ())), preferred_element_type=jnp.float32
    )


def weights_of(products, scale_value, bias_value, pair):
    same = lax.broadcasted_iota(jnp.int32, products.shape, 1) == pair
    exponent = products * (-LOG2_E * scale_value) + (-LOG2_E * bias_value)
    magnitude = scale_value / (1.0 + jnp.exp2(jnp.where(same, -exponent, exponent)))
    return jnp.where(same, -magnitude, magnitude).astype(jnp.bfloat16)


def pack_into(packed_ref, block, values):
    rows, width = values.shape
    largest = jnp.max(jnp.abs(values), axis=-1, keepdims=True)
    power = jnp.floor(jnp.log2(jnp.maximum(largest, 2.0**-100)))
    scaled = values * jnp.exp2(13.0 - power)
    lane = lax.broadcasted_iota(jnp.int32, (FOLD, LANES), 1)
    tail = jnp.zeros((FOLD, LANES), jnp.float32)
    for k in range(rows // FOLD):
        part = slice(k * FOLD, (k + 1) * FOLD)
        packed_ref[block, :, k * width : (k + 1) * width] = scaled[part, :]
        tail = jnp.where(lane == k, power[part, :], tail)
    packed_ref[block, :, rows // FOLD * width :] = tail


def block_kernel(place_ref, numbers_ref, mine_ref, other_ref, packed_ref, total_ref):
    rows = mine_ref.shape[0]
    scale_value, bias_value = numbers_ref[0], numbers_ref[1]
    places = packed_ref.shape[0]
    chip_rows = rows // places
    other = other_ref[...]
    step = rows // 2
    halves = (0, step)
    products = [products_of(mine_ref[pl.ds(start, step), :], other) for start in halves]
    for start, product in zip(halves, products):
        row = lax.broadcasted_iota(jnp.int32, (step, 1), 0) + start - place_ref[0] * chip_rows
        own = (row >= 0) & (row < chip_rows)
        pair = jnp.where(own, row + place_ref[1] * chip_rows, -1)
        weight = weights_of(product, scale_value, bias_value, pair)
        total_ref[pl.ds(start, step), :] = jnp.dot(
            weight, other, preferred_element_type=jnp.float32
        )
    for place in range(places):
        pack_into(packed_ref, place, total_ref[pl.ds(place * chip_rows, chip_rows), :])


def sum_kernel(core_ref, packed_ref, own_ref, sent_ref):
    rows, width = own_ref.shape
    folds = rows // FOLD
    totals = []
    for k in range(2 * folds):
        total = jnp.zeros((FOLD, width), jnp.float32)
        for place in range(packed_ref.shape[0]):
            factor = jnp.exp2(packed_ref[place, :, 2 * folds * width :] - 13.0)[:, k : k + 1]
            total = total + packed_ref[place, :, k * width : (k + 1) * width] * factor
        totals.append(total)
    first = core_ref[0] == 0
    for k in range(folds):
        part = pl.ds(k * FOLD, FOLD)
        own_ref[part, :] = jnp.where(first, totals[k], totals[folds + k])
        sent_ref[part, :] = jnp.where(first, totals[folds + k], totals[k])


def local(image_embed, text_embed, logit_scale, logit_bias):
    row_count, feature_count = text_embed.shape
    sizes = tuple(lax.axis_size(name) for name in MESH_AXES)
    groups = exchange_groups(sizes)
    places = len(groups[0])
    core = lax.axis_index("core")
    image_core = core == 0
    swap = [(0, 1), (1, 0)]

    def exchange(array):
        return lax.all_to_all(
            array, MESH_AXES, 0, 0, axis_index_groups=groups, tiled=True
        )

    kept, sent = lax.optimization_barrier(
        (
            jnp.where(image_core, image_embed, text_embed),
            jnp.where(image_core, text_embed, image_embed),
        )
    )
    arrived = lax.ppermute(sent, "core", swap)
    chip = jnp.concatenate(
        [jnp.where(image_core, kept, arrived), jnp.where(image_core, arrived, kept)], axis=0
    )
    mine = exchange(jnp.broadcast_to(chip[None], (places, *chip.shape)))
    mine = mine.reshape(-1, feature_count)
    other = lax.ppermute(mine, "core", swap)

    numbers = jnp.concatenate([logit_scale, logit_bias])
    x, y = lax.axis_index("x"), lax.axis_index("y")
    z_count = sizes[0] * sizes[4]
    image_place = x % 2 * z_count + lax.axis_index(("z_hi", "z_lo"))
    text_place = (x + 1) % 2 * sizes[3] + y
    place = jnp.where(
        image_core, jnp.stack([image_place, text_place]), jnp.stack([text_place, image_place])
    )
    smem = pl.BlockSpec(memory_space=pltpu.SMEM)
    vmem = pl.BlockSpec(memory_space=pltpu.VMEM)
    params = pltpu.CompilerParams(vmem_limit_bytes=24 * 2**20)
    rows = mine.shape[0]
    width = 2 * row_count // FOLD * feature_count + LANES
    packed = pl.pallas_call(
        block_kernel,
        out_shape=jax.ShapeDtypeStruct((places, FOLD, width), jnp.float32),
        in_specs=[smem, smem, vmem, vmem],
        out_specs=vmem,
        scratch_shapes=[pltpu.VMEM((rows, feature_count), jnp.float32)],
        compiler_params=params,
        cost_estimate=pl.CostEstimate(
            flops=4 * rows * rows * feature_count,
            bytes_accessed=8 * rows * feature_count,
            transcendentals=rows * rows,
        ),
        name="block",
    )(place, numbers, mine, other)
    sums = exchange(packed.astype(jnp.float16)).astype(jnp.float32)
    result = jax.ShapeDtypeStruct((row_count, feature_count), jnp.float32)
    own, sent = pl.pallas_call(
        sum_kernel,
        out_shape=(result, result),
        in_specs=[smem, vmem],
        out_specs=(vmem, vmem),
        compiler_params=params,
        cost_estimate=pl.CostEstimate(
            flops=4 * rows * feature_count,
            bytes_accessed=4 * rows * feature_count,
            transcendentals=0,
        ),
        name="sum_parts",
    )(core[None], sums)
    sibling = lax.ppermute(sent, "core", swap)
    return (jnp.where(image_core, own, sibling), jnp.where(image_core, sibling, own))


def solution(mesh):
    rows = P(MESH_AXES, None)
    return jax.shard_map(
        local,
        mesh=finer_mesh(mesh),
        in_specs=(rows, rows, P(), P()),
        out_specs=(rows, rows),
        check_vma=False,
    )
```

```python
import jax
import jax.numpy as jnp
import numpy as np
from jax import lax
from jax.experimental import pallas as pl
from jax.experimental.pallas import tpu as pltpu
from jax.sharding import Mesh, PartitionSpec as P

MESH_AXES = ("z_hi", "x", "core", "y", "z_lo")
LOG2_E = 1.4426950408889634
LANES = 128
FOLD = 8


def finer_mesh(mesh):
    return Mesh(mesh.devices.reshape(4, 4, 2, 8, 2), MESH_AXES)


def exchange_groups(sizes):
    places = np.arange(np.prod(sizes)).reshape(sizes)
    x_count, y_count = sizes[1], sizes[3]
    groups = []
    for x in range(0, x_count, 2):
        pair = [x, x + 1]
        for y in range(y_count):
            groups.append(places[:, pair, 0, y, :].transpose(1, 0, 2).reshape(-1).tolist())
    for x in range(1, x_count, 2):
        pair = [x, (x + 1) % x_count]
        for z_hi in range(sizes[0]):
            for z_lo in range(sizes[4]):
                groups.append(places[z_hi, pair, 1, :, z_lo].reshape(-1).tolist())
    return groups


def products_of(mine, other):
    return lax.dot_general(
        mine, other, (((1,), (1,)), ((), ())), preferred_element_type=jnp.float32
    )


def weights_of(products, scale_value, bias_value, pair):
    same = lax.broadcasted_iota(jnp.int32, products.shape, 1) == pair
    exponent = products * (-LOG2_E * scale_value) + (-LOG2_E * bias_value)
    magnitude = scale_value / (1.0 + jnp.exp2(jnp.where(same, -exponent, exponent)))
    return jnp.where(same, -magnitude, magnitude).astype(jnp.bfloat16)


def pack_into(packed_ref, block, values):
    rows, width = values.shape
    largest = jnp.max(jnp.abs(values), axis=-1, keepdims=True)
    power = jnp.floor(jnp.log2(jnp.maximum(largest, 2.0**-100)))
    scaled = values * jnp.exp2(13.0 - power)
    lane = lax.broadcasted_iota(jnp.int32, (FOLD, LANES), 1)
    tail = jnp.zeros((FOLD, LANES), jnp.float32)
    for k in range(rows // FOLD):
        part = slice(k * FOLD, (k + 1) * FOLD)
        packed_ref[block, :, k * width : (k + 1) * width] = scaled[part, :]
        tail = jnp.where(lane == k, power[part, :], tail)
    packed_ref[block, :, rows // FOLD * width :] = tail


def block_kernel(place_ref, numbers_ref, mine_ref, other_ref, packed_ref):
    rows = mine_ref.shape[0]
    scale_value, bias_value = numbers_ref[0], numbers_ref[1]
    places = packed_ref.shape[0]
    chip_rows = rows // places
    other = other_ref[...]
    step = rows // 2
    halves = (0, step)
    products = [products_of(mine_ref[pl.ds(start, step), :], other) for start in halves]
    for start, product in zip(halves, products):
        row = lax.broadcasted_iota(jnp.int32, (step, 1), 0) + start - place_ref[0] * chip_rows
        own = (row >= 0) & (row < chip_rows)
        pair = jnp.where(own, row + place_ref[1] * chip_rows, -1)
        weight = weights_of(product, scale_value, bias_value, pair)
        total = jnp.dot(weight, other, preferred_element_type=jnp.float32)
        for at in range(0, step, chip_rows):
            pack_into(packed_ref, (start + at) // chip_rows, total[at : at + chip_rows, :])


def sum_kernel(core_ref, packed_ref, own_ref, sent_ref):
    rows, width = own_ref.shape
    folds = rows // FOLD
    totals = []
    for k in range(2 * folds):
        total = jnp.zeros((FOLD, width), jnp.float32)
        for place in range(packed_ref.shape[0]):
            factor = jnp.exp2(packed_ref[place, :, 2 * folds * width :] - 13.0)[:, k : k + 1]
            total = total + packed_ref[place, :, k * width : (k + 1) * width] * factor
        totals.append(total)
    first = core_ref[0] == 0
    for k in range(folds):
        part = pl.ds(k * FOLD, FOLD)
        own_ref[part, :] = jnp.where(first, totals[k], totals[folds + k])
        sent_ref[part, :] = jnp.where(first, totals[folds + k], totals[k])


def local(image_embed, text_embed, logit_scale, logit_bias):
    row_count, feature_count = text_embed.shape
    sizes = tuple(lax.axis_size(name) for name in MESH_AXES)
    groups = exchange_groups(sizes)
    places = len(groups[0])
    core = lax.axis_index("core")
    image_core = core == 0
    swap = [(0, 1), (1, 0)]

    def exchange(array):
        return lax.all_to_all(
            array, MESH_AXES, 0, 0, axis_index_groups=groups, tiled=True
        )

    kept, sent = lax.optimization_barrier(
        (
            jnp.where(image_core, image_embed, text_embed),
            jnp.where(image_core, text_embed, image_embed),
        )
    )
    arrived = lax.ppermute(sent, "core", swap)
    chip = jnp.concatenate(
        [jnp.where(image_core, kept, arrived), jnp.where(image_core, arrived, kept)], axis=0
    )
    mine = exchange(jnp.broadcast_to(chip[None], (places, *chip.shape)))
    mine = mine.reshape(-1, feature_count)
    other = lax.ppermute(mine, "core", swap)

    numbers = jnp.concatenate([logit_scale, logit_bias])
    x, y = lax.axis_index("x"), lax.axis_index("y")
    z_count = sizes[0] * sizes[4]
    image_place = x % 2 * z_count + lax.axis_index(("z_hi", "z_lo"))
    text_place = (x + 1) % 2 * sizes[3] + y
    place = jnp.where(
        image_core, jnp.stack([image_place, text_place]), jnp.stack([text_place, image_place])
    )
    smem = pl.BlockSpec(memory_space=pltpu.SMEM)
    vmem = pl.BlockSpec(memory_space=pltpu.VMEM)
    params = pltpu.CompilerParams(vmem_limit_bytes=24 * 2**20)
    rows = mine.shape[0]
    width = 2 * row_count // FOLD * feature_count + LANES
    packed = pl.pallas_call(
        block_kernel,
        out_shape=jax.ShapeDtypeStruct((places, FOLD, width), jnp.float32),
        in_specs=[smem, smem, vmem, vmem],
        out_specs=vmem,
        compiler_params=params,
        cost_estimate=pl.CostEstimate(
            flops=4 * rows * rows * feature_count,
            bytes_accessed=8 * rows * feature_count,
            transcendentals=rows * rows,
        ),
        name="block",
    )(place, numbers, mine, other)
    sums = exchange(packed.astype(jnp.float16)).astype(jnp.float32)
    result = jax.ShapeDtypeStruct((row_count, feature_count), jnp.float32)
    own, sent = pl.pallas_call(
        sum_kernel,
        out_shape=(result, result),
        in_specs=[smem, vmem],
        out_specs=(vmem, vmem),
        compiler_params=params,
        cost_estimate=pl.CostEstimate(
            flops=4 * rows * feature_count,
            bytes_accessed=4 * rows * feature_count,
            transcendentals=0,
        ),
        name="sum_parts",
    )(core[None], sums)
    sibling = lax.ppermute(sent, "core", swap)
    return (jnp.where(image_core, own, sibling), jnp.where(image_core, sibling, own))


def solution(mesh):
    rows = P(MESH_AXES, None)
    return jax.shard_map(
        local,
        mesh=finer_mesh(mesh),
        in_specs=(rows, rows, P(), P()),
        out_specs=(rows, rows),
        check_vma=False,
    )
```

```python
import jax
import jax.numpy as jnp
import numpy as np
from jax import lax
from jax.experimental import pallas as pl
from jax.experimental.pallas import tpu as pltpu
from jax.sharding import Mesh, PartitionSpec as P

MESH_AXES = ("z_hi", "x", "core", "y", "z_lo")
LOG2_E = 1.4426950408889634
LANES = 128
FOLD = 8


def finer_mesh(mesh):
    return Mesh(mesh.devices.reshape(4, 4, 2, 8, 2), MESH_AXES)


def exchange_groups(sizes):
    places = np.arange(np.prod(sizes)).reshape(sizes)
    x_count, y_count = sizes[1], sizes[3]
    groups = []
    for x in range(0, x_count, 2):
        pair = [x, x + 1]
        for y in range(y_count):
            groups.append(places[:, pair, 0, y, :].transpose(0, 2, 1).reshape(-1).tolist())
    for x in range(1, x_count, 2):
        pair = [x, (x + 1) % x_count]
        for z_hi in range(sizes[0]):
            for z_lo in range(sizes[4]):
                groups.append(places[z_hi, pair, 1, :, z_lo].T.reshape(-1).tolist())
    return groups


def products_of(mine, other):
    return lax.dot_general(
        mine, other, (((1,), (1,)), ((), ())), preferred_element_type=jnp.float32
    )


def weights_of(products, scale_value, bias_value, pair):
    same = lax.broadcasted_iota(jnp.int32, products.shape, 1) == pair
    exponent = products * (-LOG2_E * scale_value) + (-LOG2_E * bias_value)
    magnitude = scale_value / (1.0 + jnp.exp2(jnp.where(same, -exponent, exponent)))
    return jnp.where(same, -magnitude, magnitude).astype(jnp.bfloat16)


def pack_into(packed_ref, block, values):
    rows, width = values.shape
    largest = jnp.max(jnp.abs(values), axis=-1, keepdims=True)
    power = jnp.floor(jnp.log2(jnp.maximum(largest, 2.0**-100)))
    scaled = values * jnp.exp2(13.0 - power)
    lane = lax.broadcasted_iota(jnp.int32, (FOLD, LANES), 1)
    tail = jnp.zeros((FOLD, LANES), jnp.float32)
    for k in range(rows // FOLD):
        part = slice(k * FOLD, (k + 1) * FOLD)
        packed_ref[block, :, k * width : (k + 1) * width] = scaled[part, :]
        tail = jnp.where(lane == k, power[part, :], tail)
    packed_ref[block, :, rows // FOLD * width :] = tail


def block_kernel(place_ref, numbers_ref, mine_ref, other_ref, packed_ref, total_ref):
    rows = mine_ref.shape[0]
    scale_value, bias_value = numbers_ref[0], numbers_ref[1]
    places = packed_ref.shape[0]
    chip_rows = rows // places
    other = other_ref[...]
    step = rows // 2
    halves = (0, step)
    products = [products_of(mine_ref[pl.ds(start, step), :], other) for start in halves]
    for start, product in zip(halves, products):
        row = lax.broadcasted_iota(jnp.int32, (step, 1), 0) + start - place_ref[0] * chip_rows
        own = (row >= 0) & (row < chip_rows)
        pair = jnp.where(own, row + place_ref[1] * chip_rows, -1)
        weight = weights_of(product, scale_value, bias_value, pair)
        total_ref[pl.ds(start, step), :] = jnp.dot(
            weight, other, preferred_element_type=jnp.float32
        )
    for place in range(places):
        pack_into(packed_ref, place, total_ref[pl.ds(place * chip_rows, chip_rows), :])


def sum_kernel(core_ref, packed_ref, own_ref, sent_ref):
    rows, width = own_ref.shape
    folds = rows // FOLD
    totals = []
    for k in range(2 * folds):
        total = jnp.zeros((FOLD, width), jnp.float32)
        for place in range(packed_ref.shape[0]):
            factor = jnp.exp2(packed_ref[place, :, 2 * folds * width :] - 13.0)[:, k : k + 1]
            total = total + packed_ref[place, :, k * width : (k + 1) * width] * factor
        totals.append(total)
    first = core_ref[0] == 0
    for k in range(folds):
        part = pl.ds(k * FOLD, FOLD)
        own_ref[part, :] = jnp.where(first, totals[k], totals[folds + k])
        sent_ref[part, :] = jnp.where(first, totals[folds + k], totals[k])


def local(image_embed, text_embed, logit_scale, logit_bias):
    row_count, feature_count = text_embed.shape
    sizes = tuple(lax.axis_size(name) for name in MESH_AXES)
    groups = exchange_groups(sizes)
    places = len(groups[0])
    core = lax.axis_index("core")
    image_core = core == 0
    swap = [(0, 1), (1, 0)]

    def exchange(array):
        return lax.all_to_all(
            array, MESH_AXES, 0, 0, axis_index_groups=groups, tiled=True
        )

    kept, sent = lax.optimization_barrier(
        (
            jnp.where(image_core, image_embed, text_embed),
            jnp.where(image_core, text_embed, image_embed),
        )
    )
    arrived = lax.ppermute(sent, "core", swap)
    chip = jnp.concatenate(
        [jnp.where(image_core, kept, arrived), jnp.where(image_core, arrived, kept)], axis=0
    )
    mine = exchange(jnp.broadcast_to(chip[None], (places, *chip.shape)))
    mine = mine.reshape(-1, feature_count)
    other = lax.ppermute(mine, "core", swap)

    numbers = jnp.concatenate([logit_scale, logit_bias])
    x, y = lax.axis_index("x"), lax.axis_index("y")
    image_place = lax.axis_index(("z_hi", "z_lo")) * 2 + x % 2
    text_place = y * 2 + (x + 1) % 2
    place = jnp.where(
        image_core, jnp.stack([image_place, text_place]), jnp.stack([text_place, image_place])
    )
    smem = pl.BlockSpec(memory_space=pltpu.SMEM)
    vmem = pl.BlockSpec(memory_space=pltpu.VMEM)
    params = pltpu.CompilerParams(vmem_limit_bytes=24 * 2**20)
    rows = mine.shape[0]
    width = 2 * row_count // FOLD * feature_count + LANES
    packed = pl.pallas_call(
        block_kernel,
        out_shape=jax.ShapeDtypeStruct((places, FOLD, width), jnp.float32),
        in_specs=[smem, smem, vmem, vmem],
        out_specs=vmem,
        scratch_shapes=[pltpu.VMEM((rows, feature_count), jnp.float32)],
        compiler_params=params,
        cost_estimate=pl.CostEstimate(
            flops=4 * rows * rows * feature_count,
            bytes_accessed=8 * rows * feature_count,
            transcendentals=rows * rows,
        ),
        name="block",
    )(place, numbers, mine, other)
    sums = exchange(packed.astype(jnp.float16)).astype(jnp.float32)
    result = jax.ShapeDtypeStruct((row_count, feature_count), jnp.float32)
    own, sent = pl.pallas_call(
        sum_kernel,
        out_shape=(result, result),
        in_specs=[smem, vmem],
        out_specs=(vmem, vmem),
        compiler_params=params,
        cost_estimate=pl.CostEstimate(
            flops=4 * rows * feature_count,
            bytes_accessed=4 * rows * feature_count,
            transcendentals=0,
        ),
        name="sum_parts",
    )(core[None], sums)
    sibling = lax.ppermute(sent, "core", swap)
    return (jnp.where(image_core, own, sibling), jnp.where(image_core, sibling, own))


def solution(mesh):
    rows = P(MESH_AXES, None)
    return jax.shard_map(
        local,
        mesh=finer_mesh(mesh),
        in_specs=(rows, rows, P(), P()),
        out_specs=(rows, rows),
        check_vma=False,
    )
```
